32 devices in a mesh: grp: 2 (over x), mem: 16 (over z, y, core).
Axes of the slice: x: 2, y: 2, z: 4, core: 2. Of those that a mesh axis runs over, the one named last changes fastest.
Arguments:
- field: bfloat16 [128, 16, 64, 256], P(('grp', 'mem')), parts along dimension 0, may hold values from -8 to 8
- norm_gain: float32 [2, 2, 256], replicated, may hold values from 0.1 to 1.9
- conv_weight: bfloat16 [2, 3, 3, 256, 512], replicated, may hold values from -0.125 to 0.125
- qkv_weight: bfloat16 [2, 256, 768], replicated, may hold values from -8 to 8
- out_weight: bfloat16 [2, 256, 256], replicated, may hold values from -0.375 to 0.375
Outputs:
- result: bfloat16 [128, 16, 64, 256], P(('grp', 'mem')), parts along dimension 0
The draws below stay inside these ranges and needn't reach their ends.
There are 2 independent parts, one for each index of `grp`. The reference program is written for one: setup_inputs(seed, part) draws one part's arguments, and reference() takes and returns one part's arrays. A program takes and returns all parts, laid end to end along the dimension named above; an argument that names none is the same for every part. Nothing has to cross between parts.
All inputs are finite; a program needn't handle non-finite values.
Results may differ from the reference program's by a relative error of at most 0.014.
Values may be sent and summed in bfloat16 or wider, within the bound.
No kernel may reach another device: no remote copies, remote signals or barrier semaphores. Data moves between devices by JAX's collectives and lax.ppermute only.
A program may use at most 128 MiB of HBM per device.

```python
import jax
import jax.numpy as jnp
from jax import lax

C = 256
HEADS = 8
BLOCKS = 2
ROWS = 16
COLS = 64
MEMBERS = 64
CELLS = 1024
N_MEM = 16


def draw_field(key, part):
    common_key = jax.random.fold_in(key, 11)
    member_key = jax.random.fold_in(key, 12)
    scale_key = jax.random.fold_in(key, 13)
    cell_key = jax.random.fold_in(key, 14)
    full_shape = (MEMBERS, ROWS, COLS, C)
    common = jax.random.normal(common_key, (1, ROWS, COLS, C), jnp.float32)
    perturb = jax.random.normal(member_key, full_shape, jnp.float32)
    cell_scale = jnp.exp(jax.random.uniform(cell_key, (1, ROWS, COLS, 1), jnp.float32, jnp.log(0.5), jnp.log(2.0)))
    member_scale = jnp.exp(jax.random.uniform(scale_key, (MEMBERS, 1, 1, 1), jnp.float32, jnp.log(0.3), jnp.log(1.5)))
    return jnp.clip((common + member_scale * perturb) * cell_scale, -8.0, 8.0).astype(jnp.bfloat16)


def draw_qkv_weight(key, part):
    weight_key = jax.random.fold_in(key, 21)
    baseline = jax.random.normal(weight_key, (BLOCKS, C, 3 * C), jnp.float32) * C ** (-0.5)
    return jnp.clip(baseline, -8.0, 8.0).astype(jnp.bfloat16)


def gaussian(rng, shape, spread, most, dtype=jnp.bfloat16):
    drawn = jax.random.normal(rng, shape, jnp.float32) * spread
    return jnp.minimum(jnp.maximum(drawn, -most), most).astype(dtype)


def setup_inputs(seed: int = 0, part: int = 0) -> dict:
    streams_of = jax.random.split(jax.random.key(seed), 6)
    part_keys = jax.random.split(jax.random.fold_in(streams_of[5], part), 6)
    return {
        "field": draw_field(jax.random.fold_in(jax.random.fold_in(streams_of[5], part), 71), part),
        "norm_gain": jnp.clip(1.0 + 0.18 * jax.random.normal(streams_of[1], (BLOCKS, 2, C), jnp.float32), 0.1, 1.9),
        "conv_weight": gaussian(streams_of[2], (BLOCKS, 3, 3, C, 2 * C), (9 * C) ** -0.5, 0.125),
        "qkv_weight": draw_qkv_weight(jax.random.fold_in(streams_of[5], 71), part),
        "out_weight": gaussian(streams_of[4], (BLOCKS, C, C), C ** -0.5, 0.375),
    }


epsilon = 1e-06

def rounded(values):
    return lax.optimization_barrier(values.astype(jnp.bfloat16))

def rms_norm(hidden_state, gain_row):
    widened = hidden_state.astype(jnp.float32)
    inverse = lax.rsqrt(lax.optimization_barrier(jnp.mean(widened * widened, axis=-1, keepdims=True)) + epsilon)
    return rounded(widened * inverse * gain_row)

def attend(cell_group, channels):
    head_size = channels // HEADS
    all_members, group_cells, _ = cell_group.shape
    widened = cell_group.astype(jnp.float32)
    queries = widened[:, :, :channels].reshape(all_members, group_cells, HEADS, head_size)
    keys_split = widened[:, :, channels:2 * channels].reshape(all_members, group_cells, HEADS, head_size)
    values_split = widened[:, :, 2 * channels:].reshape(all_members, group_cells, HEADS, head_size)
    scores = jnp.einsum('mchd,nchd->chmn', queries, keys_split, precision=lax.Precision.HIGHEST) * head_size ** (-0.5)
    row_max = lax.optimization_barrier(jnp.max(scores, axis=-1, keepdims=True))
    expo = jnp.exp(scores - row_max)
    probs = rounded(expo / lax.optimization_barrier(jnp.sum(expo, axis=-1, keepdims=True))).astype(jnp.float32)
    mixed = jnp.einsum('chmn,nchd->mchd', probs, values_split, precision=lax.Precision.HIGHEST)
    return rounded(mixed.reshape(all_members, group_cells, channels))

def reference(field, norm_gain, conv_weight, qkv_weight, out_weight):
    hidden_state = field
    channels = field.shape[-1]
    for layer_index in range(BLOCKS):
        normed = rms_norm(hidden_state, norm_gain[layer_index, 0])
        conv_out = lax.conv_general_dilated(normed.astype(jnp.float32), conv_weight[layer_index].astype(jnp.float32), (1, 1), 'SAME', dimension_numbers=('NHWC', 'HWIO', 'NHWC'), precision=lax.Precision.HIGHEST)
        value_part = conv_out[..., :channels]
        gate_part = conv_out[..., channels:]
        hidden_state = (hidden_state.astype(jnp.float32) + value_part * jax.nn.sigmoid(gate_part)).astype(jnp.bfloat16)
        normed2 = rms_norm(hidden_state, norm_gain[layer_index, 1]).reshape(MEMBERS * CELLS, channels)
        projected = rounded(jnp.dot(normed2, qkv_weight[layer_index], preferred_element_type=jnp.float32))
        grouped = projected.reshape(MEMBERS, N_MEM, CELLS // N_MEM, 3 * channels).transpose(1, 0, 2, 3)
        attended = lax.map(lambda cell_group: attend(cell_group, channels), grouped)
        attended = attended.transpose(1, 0, 2, 3).reshape(MEMBERS * CELLS, channels)
        update = jnp.dot(attended, out_weight[layer_index], preferred_element_type=jnp.float32)
        hidden_state = (hidden_state.astype(jnp.float32) + update.reshape(hidden_state.shape)).astype(jnp.bfloat16)
    return hidden_state
```

```python
import functools

import jax
import jax.numpy as jnp
import numpy as np
from jax import lax
from jax.experimental import pallas as pl
from jax.experimental.pallas import tpu as pltpu
from jax.sharding import PartitionSpec as P

HEADS = 8
BLOCKS = 2
LANES = 128
epsilon = 1e-06
VMEM_LIMIT = 48 * 1024 * 1024

F32 = jnp.float32
BF16 = jnp.bfloat16


def tile_of(device, count):
    if count % 4:
        return device
    group, inner = device // 4, device % 4
    if group % 2:
        inner = (2, 3, 0, 1)[inner]
    return group * 4 + inner


def one_hot(sources):
    matrix = np.zeros((len(sources), len(sources)), np.float32)
    matrix[np.arange(len(sources)), np.asarray(sources)] = 1.0
    return jnp.asarray(matrix, BF16)


def shuffles(count, local, cols):
    width = cols // count
    members = count * local
    tiles = [tile_of(d, count) for d in range(count)]
    to_message = [
        m * cols + tiles[d] * width + c
        for d in range(count)
        for m in range(local)
        for c in range(width)
    ]
    to_slab = np.argsort(to_message)
    to_tile = [
        d * local * width + m * width + c
        for c in range(width)
        for d in range(count)
        for m in range(local)
    ]
    from_tile = np.argsort(to_tile)
    return one_hot(to_message), one_hot(to_tile), one_hot(from_tile), one_hot(to_slab)


def normalize(widened, gain):
    inverse = lax.rsqrt(jnp.mean(widened * widened, axis=-1, keepdims=True) + epsilon)
    return widened * inverse * gain


def gated(conv_out, channels):
    return conv_out[:, :channels] * jax.nn.sigmoid(conv_out[:, channels:])


def shuffled(matrix, rows):
    return jnp.dot(matrix, rows, preferred_element_type=F32)


def attention_rows(state, gain, wqv_t, wk, wout, members):
    count, channels = state.shape
    size = channels // HEADS
    group = LANES // size
    packed = LANES // members
    factor = float(np.log2(np.e) / np.sqrt(size))
    normed = normalize(state, gain).astype(BF16)
    keys = jnp.dot(normed, wk, preferred_element_type=F32).astype(BF16)
    qv_t = lax.dot_general(
        wqv_t, normed, (((1,), (1,)), ((), ())), preferred_element_type=F32
    ).astype(BF16)
    lane = lax.broadcasted_iota(jnp.int32, (members, LANES), 1)
    columns = []
    for j in range(count // LANES):
        span = slice(j * LANES, (j + 1) * LANES)
        pieces = []
        for q in range(channels // LANES):
            blocks = []
            for h in range(group):
                row = q * LANES + h * size
                parts = [jnp.zeros((size, LANES), BF16)] * group
                parts[h] = qv_t[row : row + size, span]
                blocks.append(jnp.concatenate(parts, axis=1))
            spread = jnp.concatenate(blocks, axis=0)
            scores = jnp.dot(
                keys[span, q * LANES : (q + 1) * LANES], spread, preferred_element_type=F32
            )
            for h in range(group):
                square = scores[:, h * LANES : (h + 1) * LANES]
                dense = square[:members]
                for k in range(1, packed):
                    dense = jnp.where(
                        lane < k * members, dense, square[k * members : (k + 1) * members]
                    )
                top = jnp.max(dense, axis=0, keepdims=True)
                expo = jnp.exp2((dense - top) * factor)
                total = jnp.sum(expo, axis=0, keepdims=True)
                if packed == 1:
                    weights = expo.astype(BF16)
                else:
                    weights = jnp.concatenate(
                        [
                            jnp.where(
                                (lane >= k * members) & (lane < (k + 1) * members), expo, 0.0
                            ).astype(BF16)
                            for k in range(packed)
                        ],
                        axis=0,
                    )
                row = channels + q * LANES + h * size
                mixed = jnp.dot(
                    qv_t[row : row + size, span], weights, preferred_element_type=F32
                )
                pieces.append((mixed * (1.0 / total)).astype(BF16))
        columns.append(jnp.concatenate(pieces, axis=0))
    attended_t = jnp.concatenate(columns, axis=1)
    update = lax.dot_general(
        attended_t, wout, (((0,), (0,)), ((), ())), preferred_element_type=F32
    )
    return state + update


def conv_slab_kernel(first, last, field_ref, gain_ref, weight_ref, order_ref, out_ref, padded):
    local, rows, cols, channels = field_ref.shape
    count = local * cols
    column = lax.broadcasted_iota(jnp.int32, (count, 1), 0) % cols

    def prepare(slot, row):
        widened = field_ref[:, row].reshape(count, channels).astype(F32)
        normed = normalize(widened, gain_ref[...])
        left = jnp.where(column == 0, 0.0, pltpu.roll(normed, 1, 0))
        right = jnp.where(column == cols - 1, 0.0, pltpu.roll(normed, count - 1, 0))
        padded[slot, 0] = left.astype(BF16)
        padded[slot, 1] = normed.astype(BF16)
        padded[slot, 2] = right.astype(BF16)

    total = last - first
    low = 1 if first == 0 else 0
    high = total + 1 if last == rows else total + 2
    if low:
        padded[0] = jnp.zeros(padded.shape[1:], BF16)
    if high < total + 2:
        padded[total + 1] = jnp.zeros(padded.shape[1:], BF16)

    def prepare_step(slot, carry):
        prepare(slot, slot + (first - 1))
        return carry

    lax.fori_loop(low, high, prepare_step, 0)

    def step(i, carry):
        taps = [padded[i + di, dj] for di in range(3) for dj in range(3)]
        conv_out = jnp.dot(
            jnp.concatenate(taps, axis=1), weight_ref[...], preferred_element_type=F32
        )
        widened = field_ref[:, first + i].reshape(count, channels).astype(F32)
        state = (widened + gated(conv_out, channels)).astype(BF16)
        moved = shuffled(order_ref[...], state)
        out_ref[:, i] = moved.reshape(out_ref.shape[0], out_ref.shape[2], channels).astype(BF16)
        return carry

    lax.fori_loop(0, total, step, 0)


def attend_kernel(
    members, arrived_ref, gain_ref, next_gain_ref, wqv_ref, wk_ref, wout_ref, order_ref,
    state_ref, normed_ref, low_ref, high_ref,
):
    channels = state_ref.shape[-1]
    count = state_ref.shape[1]
    rows = arrived_ref[:, 0].reshape(count, channels)
    state = shuffled(order_ref[...], rows)
    state = attention_rows(
        state, gain_ref[...], wqv_ref[...], wk_ref[...], wout_ref[...], members
    ).astype(BF16)
    state_ref[0] = state
    normed = normalize(state.astype(F32), next_gain_ref[...]).astype(BF16)
    normed_ref[0] = normed
    low_ref[0] = normed[:members]
    high_ref[0] = normed[count - members :]


def conv_tile_kernel(
    first, last, rows, spans, members, *refs,
):
    pieces = len(spans)
    states, normeds = refs[:pieces], refs[pieces : 2 * pieces]
    lows, highs = refs[2 * pieces : 3 * pieces], refs[3 * pieces : 4 * pieces]
    weight_ref, gain_ref, wqv_ref, wk_ref, wout_ref, order_ref, out_ref, padded, held = refs[
        4 * pieces :
    ]
    count, channels = states[0].shape[1:]
    total = last - first
    if first == 0:
        padded[0] = jnp.zeros(padded.shape[1:], BF16)
    if last == rows:
        padded[total + 1] = jnp.zeros(padded.shape[1:], BF16)
    for k, (begin, end) in enumerate(spans):
        begin_row, end_row = max(begin, first - 1), min(end, last + 1)
        for row in range(begin_row, end_row):
            slot = row - first + 1
            padded[slot, :members] = lows[k][row - begin]
            padded[slot, members : members + count] = normeds[k][row - begin]
            padded[slot, members + count :] = highs[k][row - begin]
            if first <= row < last:
                held[row - first] = states[k][row - begin]

    def step(i, carry):
        taps = [
            padded[i + di, dj * members : dj * members + count]
            for di in range(3)
            for dj in range(3)
        ]
        conv_out = jnp.dot(
            jnp.concatenate(taps, axis=1), weight_ref[...], preferred_element_type=F32
        )
        state = (held[i].astype(F32) + gated(conv_out, channels)).astype(BF16).astype(F32)
        state = attention_rows(
            state, gain_ref[...], wqv_ref[...], wk_ref[...], wout_ref[...], members
        ).astype(BF16)
        moved = shuffled(order_ref[...], state)
        out_ref[:, i] = moved.reshape(out_ref.shape[0], out_ref.shape[2], channels).astype(BF16)
        return carry

    lax.fori_loop(0, total, step, 0)


def place_kernel(arrived_ref, order_ref, *refs):
    out_ref = refs[-1]
    local, _, cols, channels = out_ref.shape
    rows = arrived_ref[:, 0].reshape(local * cols, channels)
    moved = shuffled(order_ref[...], rows)
    out_ref[:, 0] = moved.reshape(local, cols, channels).astype(BF16)


def params():
    return pltpu.CompilerParams(vmem_limit_bytes=VMEM_LIMIT)


def whole():
    return pl.BlockSpec(memory_space=pltpu.VMEM)


def body(field, norm_gain, conv_weight, qkv_weight, out_weight):
    local, rows, cols, channels = field.shape
    devices = lax.axis_size("mem")
    width = cols // devices
    members = devices * local
    count = local * cols
    block = local * width
    to_message, to_tile, from_tile, to_slab = shuffles(devices, local, cols)
    taps = conv_weight.shape[1] * conv_weight.shape[2] * channels
    conv_weight = conv_weight.reshape(BLOCKS, taps, 2 * channels)
    wk = qkv_weight[:, :, channels : 2 * channels]
    wqv_t = jnp.concatenate(
        [qkv_weight[:, :, :channels], qkv_weight[:, :, 2 * channels :]], axis=2
    ).transpose(0, 2, 1)
    gains = norm_gain.reshape(BLOCKS, 2, 1, channels)

    split_in = rows // 2 + 1
    split_out = split_in - 1
    spans_in = ((0, split_in), (split_in, rows))
    spans_out = ((0, split_out), (split_out, rows))

    def conv_slab(first, last):
        total = last - first
        return pl.pallas_call(
            functools.partial(conv_slab_kernel, first, last),
            out_shape=jax.ShapeDtypeStruct((devices, total, block, channels), BF16),
            in_specs=[whole()] * 4,
            out_specs=whole(),
            scratch_shapes=[pltpu.VMEM((total + 2, 3, count, channels), BF16)],
            compiler_params=params(),
            cost_estimate=pl.CostEstimate(
                flops=2 * total * count * taps * 2 * channels,
                bytes_accessed=2 * total * count * channels * 2,
                transcendentals=total * count * channels,
            ),
            name="conv_slab",
        )(field, gains[0, 0], conv_weight[0], to_message)

    def exchange(messages):
        return lax.all_to_all(messages, "mem", split_axis=0, concat_axis=0, tiled=True)

    def attend(arrived):
        total = arrived.shape[1]
        fixed = lambda shape: pl.BlockSpec(shape, lambda i: (0,) * len(shape))
        per_row = lambda n: pl.BlockSpec((1, n, channels), lambda i: (i, 0, 0))
        return pl.pallas_call(
            functools.partial(attend_kernel, members),
            grid=(total,),
            out_shape=[
                jax.ShapeDtypeStruct((total, count, channels), BF16),
                jax.ShapeDtypeStruct((total, count, channels), BF16),
                jax.ShapeDtypeStruct((total, members, channels), BF16),
                jax.ShapeDtypeStruct((total, members, channels), BF16),
            ],
            in_specs=[
                pl.BlockSpec((devices, 1, block, channels), lambda i: (0, i, 0, 0)),
                fixed((1, channels)),
                fixed((1, channels)),
                fixed((2 * channels, channels)),
                fixed((channels, channels)),
                fixed((channels, channels)),
                fixed((count, count)),
            ],
            out_specs=[per_row(count), per_row(count), per_row(members), per_row(members)],
            compiler_params=params(),
            cost_estimate=pl.CostEstimate(
                flops=2 * total * count * channels * 6 * channels,
                bytes_accessed=4 * total * count * channels * 2,
                transcendentals=total * count * members * HEADS,
            ),
            name="attend",
        )(arrived, gains[0, 1], gains[1, 0], wqv_t[0], wk[0], out_weight[0], to_tile)

    tiles = [tile_of(d, devices) for d in range(devices)]
    owner = {t: d for d, t in enumerate(tiles)}
    rightward = [(owner[t], owner[t + 1]) for t in range(devices - 1)]
    leftward = [(target, source) for source, target in rightward]

    def conv_tile(first, last, spans, parts):
        total = last - first
        operands = [p[k] for k in range(4) for p in parts]
        return pl.pallas_call(
            functools.partial(conv_tile_kernel, first, last, rows, spans, members),
            out_shape=jax.ShapeDtypeStruct((devices, total, block, channels), BF16),
            in_specs=[whole()] * (len(operands) + 6),
            out_specs=whole(),
            scratch_shapes=[
                pltpu.VMEM((total + 2, count + 2 * members, channels), BF16),
                pltpu.VMEM((total, count, channels), BF16),
            ],
            compiler_params=params(),
            cost_estimate=pl.CostEstimate(
                flops=2 * total * count * channels * (6 * channels + 2 * taps),
                bytes_accessed=4 * total * count * channels * 2,
                transcendentals=total * count * members * HEADS,
            ),
            name="conv_tile",
        )(
            *operands, conv_weight[1], gains[1, 1], wqv_t[1], wk[1], out_weight[1], from_tile,
        )

    def place(first, last, arrived, earlier):
        total = last - first
        in_specs = [
            pl.BlockSpec((devices, 1, block, channels), lambda i: (0, i, 0, 0)),
            pl.BlockSpec((count, count), lambda i: (0, 0)),
        ]
        operands = [arrived, to_slab]
        aliases = {}
        if earlier is not None:
            in_specs.append(pl.BlockSpec(memory_space=pl.ANY))
            operands.append(earlier)
            aliases = {2: 0}
        return pl.pallas_call(
            place_kernel,
            grid=(total,),
            out_shape=jax.ShapeDtypeStruct((local, rows, cols, channels), BF16),
            in_specs=in_specs,
            out_specs=pl.BlockSpec(
                (local, 1, cols, channels), lambda i: (0, first + i, 0, 0)
            ),
            input_output_aliases=aliases,
            compiler_params=params(),
            cost_estimate=pl.CostEstimate(
                flops=2 * total * count * count * channels,
                bytes_accessed=2 * total * count * channels * 2,
                transcendentals=0,
            ),
            name="place",
        )(*operands)

    arrived = [exchange(conv_slab(*span)) for span in spans_in]
    parts = []
    result = None
    for k, (first, last) in enumerate(spans_out):
        state, normed, low, high = attend(arrived[k])
        from_left = lax.ppermute(high, "mem", rightward)
        from_right = lax.ppermute(low, "mem", leftward)
        parts.append((state, normed, from_left, from_right))
    returned = []
    for k, (first, last) in enumerate(spans_out):
        lo = 0 if k == 0 else k - 1
        spans = spans_in[lo : k + 1]
        messages = conv_tile(first, last, spans, parts[lo : k + 1])
        returned.append(exchange(messages))
    for span, arrival in zip(spans_out, returned):
        result = place(*span, arrival, result)
    return result


def solution(mesh):
    return jax.shard_map(
        body,
        mesh=mesh,
        in_specs=(P(("grp", "mem"), None, None, None), P(), P(), P(), P()),
        out_specs=P(("grp", "mem"), None, None, None),
        check_vma=False,
    )
```

```python
import functools

import jax
import jax.numpy as jnp
import numpy as np
from jax import lax
from jax.experimental import pallas as pl
from jax.experimental.pallas import tpu as pltpu
from jax.sharding import PartitionSpec as P

HEADS = 8
BLOCKS = 2
LANES = 128
epsilon = 1e-06
VMEM_LIMIT = 60 * 1024 * 1024
UNROLL = 4

F32 = jnp.float32
BF16 = jnp.bfloat16


def tile_of(device, count):
    if count % 4:
        return device
    group, inner = device // 4, device % 4
    if group % 2:
        inner = (2, 3, 0, 1)[inner]
    return group * 4 + inner


def one_hot(sources):
    matrix = np.zeros((len(sources), len(sources)), np.float32)
    matrix[np.arange(len(sources)), np.asarray(sources)] = 1.0
    return jnp.asarray(matrix, BF16)


def shuffles(count, local, cols):
    width = cols // count
    members = count * local
    tiles = [tile_of(d, count) for d in range(count)]
    to_message = [
        m * cols + tiles[d] * width + c
        for d in range(count)
        for m in range(local)
        for c in range(width)
    ]
    to_slab = np.argsort(to_message)
    to_tile = [
        d * local * width + m * width + c
        for c in range(width)
        for d in range(count)
        for m in range(local)
    ]
    from_tile = np.argsort(to_tile)
    return one_hot(to_message), one_hot(to_tile), one_hot(from_tile), one_hot(to_slab)


def normalize(widened, gain):
    inverse = lax.rsqrt(jnp.mean(widened * widened, axis=-1, keepdims=True) + epsilon)
    return widened * inverse * gain


def gated(conv_out, channels):
    return conv_out[:, :channels] * jax.nn.sigmoid(conv_out[:, channels:])


def shuffled(matrix, rows):
    return jnp.dot(matrix, rows, preferred_element_type=F32)


def groups_of(total, most=UNROLL):
    pieces = -(-total // most)
    edges = [total * k // pieces for k in range(pieces + 1)]
    return [(edges[k], edges[k + 1]) for k in range(pieces)]


def attention_rows(state, gain, wqv_t, wk, wout, members, count):
    total, channels = state.shape
    size = channels // HEADS
    group = LANES // size
    packed = LANES // members
    factor = float(np.log2(np.e) / np.sqrt(size))
    normed = normalize(state, gain).astype(BF16)
    keys = jnp.dot(normed, wk, preferred_element_type=F32).astype(BF16)
    qv_t = lax.dot_general(
        wqv_t, normed, (((1,), (1,)), ((), ())), preferred_element_type=F32
    ).astype(BF16)
    lane = lax.broadcasted_iota(jnp.int32, (members, LANES), 1)
    masks = [
        ((lane >= k * members) & (lane < (k + 1) * members)).astype(F32).astype(BF16)
        for k in range(packed)
    ]
    spans = [slice(j * LANES, (j + 1) * LANES) for j in range(total // LANES)]
    quads = range(channels // LANES)
    scores = {}
    for j, span in enumerate(spans):
        for q in quads:
            blocks = []
            for h in range(group):
                row = q * LANES + h * size
                parts = [jnp.zeros((size, LANES), BF16)] * group
                parts[h] = qv_t[row : row + size, span]
                blocks.append(jnp.concatenate(parts, axis=1))
            scores[j, q] = jnp.dot(
                keys[span, q * LANES : (q + 1) * LANES],
                jnp.concatenate(blocks, axis=0),
                preferred_element_type=F32,
            )
    weights = {}
    for j in range(len(spans)):
        for q in quads:
            for h in range(group):
                square = scores[j, q][:, h * LANES : (h + 1) * LANES]
                dense = square[:members]
                for k in range(1, packed):
                    dense = jnp.where(
                        lane < k * members, dense, square[k * members : (k + 1) * members]
                    )
                top = jnp.max(dense, axis=0, keepdims=True)
                expo = jnp.exp2((dense - top) * factor)
                inverse = 1.0 / jnp.sum(expo, axis=0, keepdims=True)
                spread = expo.astype(BF16)
                if packed > 1:
                    spread = jnp.concatenate([spread * mask for mask in masks], axis=0)
                weights[j, q, h] = spread, inverse
    columns = []
    for j, span in enumerate(spans):
        pieces = []
        for q in quads:
            for h in range(group):
                spread, inverse = weights[j, q, h]
                row = channels + q * LANES + h * size
                mixed = jnp.dot(
                    qv_t[row : row + size, span], spread, preferred_element_type=F32
                )
                pieces.append((mixed * inverse).astype(BF16))
        columns.append(jnp.concatenate(pieces, axis=0))
    attended_t = jnp.concatenate(columns, axis=1)
    update = lax.dot_general(
        attended_t, wout, (((0,), (0,)), ((), ())), preferred_element_type=F32
    )
    return state + update


class Copies:
    def __init__(self, semaphores):
        self.semaphores = semaphores
        self.used = 0

    def start(self, source, target):
        copy = pltpu.make_async_copy(source, target, self.semaphores.at[self.used])
        self.used += 1
        copy.start()
        return copy


def wait_all(copies):
    for copy in copies:
        copy.wait()


def split_weights(qkv, wqv_t):
    channels = qkv.shape[0]
    wqv_t[:channels] = qkv[:, :channels].T
    wqv_t[channels:] = qkv[:, 2 * channels :].T


def conv_slab_kernel(
    layer, first, last, field_hbm, gain_hbm, weight_hbm, order_hbm, out_hbm,
    field, gain, weight, order, padded, out, semaphores,
):
    local, rows, cols, channels = field_hbm.shape
    count = local * cols
    copies = Copies(semaphores)
    low, high = max(first - 1, 0), min(last + 1, rows)
    inputs = [
        copies.start(gain_hbm, gain),
        copies.start(field_hbm.at[:, low:high], field),
    ]
    late = [
        copies.start(weight_hbm.at[layer], weight),
        copies.start(order_hbm, order),
    ]
    column = lax.broadcasted_iota(jnp.int32, (count, 1), 0) % cols
    zeros = jnp.zeros(padded.shape[1:], BF16)
    if first == 0:
        padded[0] = zeros
    if last == rows:
        padded[last - first + 1] = zeros
    wait_all(inputs)
    gain_row = gain[layer, 0:1]

    def prepare(row):
        widened = field[:, row - low].reshape(count, channels).astype(F32)
        normed = normalize(widened, gain_row)
        left = jnp.where(column == 0, 0.0, pltpu.roll(normed, 1, 0))
        right = jnp.where(column == cols - 1, 0.0, pltpu.roll(normed, count - 1, 0))
        slot = row - first + 1
        padded[slot, 0] = left.astype(BF16)
        padded[slot, 1] = normed.astype(BF16)
        padded[slot, 2] = right.astype(BF16)

    ready = low
    outputs = []
    for k, (begin, end) in enumerate(groups_of(last - first)):
        needed = min(first + end + 1, rows)
        for row in range(ready, needed):
            prepare(row)
        ready = needed
        if k == 0:
            wait_all(late)
        taps = [
            jnp.concatenate(
                [padded[i + di, dj] for di in range(3) for dj in range(3)], axis=1
            )
            for i in range(begin, end)
        ]
        conv_out = jnp.dot(
            jnp.concatenate(taps, axis=0),
            weight[...].reshape(9 * channels, 2 * channels),
            preferred_element_type=F32,
        )
        update = gated(conv_out, channels)
        for i in range(begin, end):
            widened = field[:, first + i - low].reshape(count, channels).astype(F32)
            part = update[(i - begin) * count : (i - begin + 1) * count]
            moved = shuffled(order[...], (widened + part).astype(BF16))
            out[:, i] = moved.reshape(out.shape[0], out.shape[2], channels).astype(BF16)
        outputs.append(copies.start(out.at[:, begin:end], out_hbm.at[:, begin:end]))
    wait_all(outputs)


def attend_kernel(
    layer, members, arrived_hbm, gain_hbm, qkv_hbm, wout_hbm, order_hbm,
    state_hbm, normed_hbm, low_hbm, high_hbm,
    arrived, gain, qkv, wqv_t, wout, order, state, normed, semaphores,
):
    total, count, channels = state.shape
    groups = groups_of(total)
    copies = Copies(semaphores)
    inputs = [
        copies.start(qkv_hbm.at[layer], qkv),
        copies.start(gain_hbm, gain),
        copies.start(order_hbm, order),
        copies.start(wout_hbm.at[layer], wout),
    ]
    rows_in = [
        copies.start(arrived_hbm.at[:, begin:end], arrived.at[:, begin:end])
        for begin, end in groups
    ]
    wait_all(inputs)
    split_weights(qkv, wqv_t)
    outputs = []
    for (begin, end), copy in zip(groups, rows_in):
        copy.wait()
        joined = jnp.concatenate(
            [
                shuffled(order[...], arrived[:, i].reshape(count, channels))
                for i in range(begin, end)
            ],
            axis=0,
        )
        joined = attention_rows(
            joined, gain[layer, 1:2], wqv_t[...], qkv[:, channels : 2 * channels], wout[...],
            members, count,
        ).astype(BF16)
        following = normalize(joined.astype(F32), gain[layer + 1, 0:1]).astype(BF16)
        for i in range(begin, end):
            span = slice((i - begin) * count, (i - begin + 1) * count)
            state[i] = joined[span]
            normed[i] = following[span]
        part = slice(begin, end)
        outputs += [
            copies.start(state.at[part], state_hbm.at[part]),
            copies.start(normed.at[part], normed_hbm.at[part]),
            copies.start(normed.at[part, :members], low_hbm.at[part]),
            copies.start(normed.at[part, count - members :], high_hbm.at[part]),
        ]
    wait_all(outputs)


def conv_tile_kernel(layer, first, last, rows, spans, members, *refs):
    pieces = len(spans)
    states, normeds = refs[:pieces], refs[pieces : 2 * pieces]
    lows, highs = refs[2 * pieces : 3 * pieces], refs[3 * pieces : 4 * pieces]
    (
        weight_hbm, gain_hbm, qkv_hbm, wout_hbm, order_hbm, out_hbm,
        padded, held, weight, gain, qkv, wqv_t, wout, order, out, semaphores,
    ) = refs[4 * pieces :]
    total, count, channels = held.shape
    copies = Copies(semaphores)
    inputs = []
    for k, (begin, end) in enumerate(spans):
        lo, hi = max(begin, first - 1), min(end, last + 1)
        source, slots = slice(lo - begin, hi - begin), slice(lo - first + 1, hi - first + 1)
        inputs += [
            copies.start(normeds[k].at[source], padded.at[slots, members : members + count]),
            copies.start(lows[k].at[source], padded.at[slots, :members]),
            copies.start(highs[k].at[source], padded.at[slots, members + count :]),
        ]
    inputs.append(copies.start(weight_hbm.at[layer], weight))
    late = [
        copies.start(qkv_hbm.at[layer], qkv),
        copies.start(gain_hbm, gain),
        copies.start(order_hbm, order),
        copies.start(wout_hbm.at[layer], wout),
    ]
    for k, (begin, end) in enumerate(spans):
        lo, hi = max(begin, first), min(end, last)
        if lo < hi:
            late.append(
                copies.start(states[k].at[lo - begin : hi - begin], held.at[lo - first : hi - first])
            )
    zeros = jnp.zeros(padded.shape[1:], BF16)
    if first == 0:
        padded[0] = zeros
    if last == rows:
        padded[total + 1] = zeros
    wait_all(late)
    split_weights(qkv, wqv_t)
    wait_all(inputs)
    outputs = []
    for begin, end in groups_of(total):
        taps = [
            jnp.concatenate(
                [
                    padded[i + di, dj * members : dj * members + count]
                    for di in range(3)
                    for dj in range(3)
                ],
                axis=1,
            )
            for i in range(begin, end)
        ]
        conv_out = jnp.dot(
            jnp.concatenate(taps, axis=0),
            weight[...].reshape(9 * channels, 2 * channels),
            preferred_element_type=F32,
        )
        joined = held[begin:end].reshape((end - begin) * count, channels).astype(F32)
        joined = (joined + gated(conv_out, channels)).astype(BF16).astype(F32)
        joined = attention_rows(
            joined, gain[layer, 1:2], wqv_t[...], qkv[:, channels : 2 * channels], wout[...],
            members, count,
        ).astype(BF16)
        for i in range(begin, end):
            moved = shuffled(order[...], joined[(i - begin) * count : (i - begin + 1) * count])
            out[:, i] = moved.reshape(out.shape[0], out.shape[2], channels).astype(BF16)
        outputs.append(copies.start(out.at[:, begin:end], out_hbm.at[:, begin:end]))
    wait_all(outputs)


def place_kernel(first, arrived_hbm, order_hbm, *refs):
    out_hbm, arrived, order, out, semaphores = refs[-5:]
    local, total, cols, channels = out.shape
    copies = Copies(semaphores)
    inputs = [copies.start(order_hbm, order)]
    groups = groups_of(total)
    rows_in = [
        copies.start(arrived_hbm.at[:, begin:end], arrived.at[:, begin:end])
        for begin, end in groups
    ]
    wait_all(inputs)
    outputs = []
    for (begin, end), copy in zip(groups, rows_in):
        copy.wait()
        for i in range(begin, end):
            moved = shuffled(order[...], arrived[:, i].reshape(local * cols, channels))
            out[:, i] = moved.reshape(local, cols, channels).astype(BF16)
        outputs.append(
            copies.start(out.at[:, begin:end], out_hbm.at[:, first + begin : first + end])
        )
    wait_all(outputs)


def anywhere():
    return pl.BlockSpec(memory_space=pl.ANY)


def call(kernel, name, operands, outs, scratch, flops, moved, transcendentals=0, aliases=None):
    return pl.pallas_call(
        kernel,
        out_shape=[jax.ShapeDtypeStruct(shape, BF16) for shape in outs],
        in_specs=[anywhere()] * len(operands),
        out_specs=[anywhere()] * len(outs),
        scratch_shapes=[pltpu.VMEM(shape, dtype) for shape, dtype in scratch]
        + [pltpu.SemaphoreType.DMA((48,))],
        input_output_aliases=aliases or {},
        compiler_params=pltpu.CompilerParams(vmem_limit_bytes=VMEM_LIMIT),
        cost_estimate=pl.CostEstimate(
            flops=flops, bytes_accessed=moved, transcendentals=transcendentals
        ),
        name=name,
    )(*operands)


def body(field, norm_gain, conv_weight, qkv_weight, out_weight):
    local, rows, cols, channels = field.shape
    devices = lax.axis_size("mem")
    width = cols // devices
    members = devices * local
    count = local * cols
    block = local * width
    to_message, to_tile, from_tile, to_slab = shuffles(devices, local, cols)
    taps = conv_weight.shape[1] * conv_weight.shape[2] * channels
    conv_shape = conv_weight.shape[1:]
    gain_shape = norm_gain.shape

    split_in = rows // 2 + 1
    split_out = split_in - 1
    spans_in = ((0, split_in), (split_in, rows))
    spans_out = ((0, split_out), (split_out, rows))

    square = ((count, count), BF16)
    attention_weights = [
        (gain_shape, F32),
        ((channels, 3 * channels), BF16),
        ((2 * channels, channels), BF16),
        ((channels, channels), BF16),
        square,
    ]

    def conv_slab(first, last):
        total = last - first
        held = min(last + 1, rows) - max(first - 1, 0)
        messages = (devices, total, block, channels)
        return call(
            functools.partial(conv_slab_kernel, 0, first, last),
            "conv_slab",
            (field, norm_gain, conv_weight, to_message),
            [messages],
            [
                ((local, held, cols, channels), BF16),
                (gain_shape, F32),
                (conv_shape, BF16),
                square,
                ((total + 2, 3, count, channels), BF16),
                (messages, BF16),
            ],
            2 * total * count * taps * 2 * channels,
            4 * total * count * channels,
            total * count * channels,
        )[0]

    def exchange(messages):
        return lax.all_to_all(messages, "mem", split_axis=0, concat_axis=0, tiled=True)

    def attend(arrived):
        total = arrived.shape[1]
        whole, edge = (total, count, channels), (total, members, channels)
        return call(
            functools.partial(attend_kernel, 0, members),
            "attend",
            (arrived, norm_gain, qkv_weight, out_weight, to_tile),
            [whole, whole, edge, edge],
            [(arrived.shape, BF16)] + attention_weights + [(whole, BF16), (whole, BF16)],
            2 * total * count * channels * 6 * channels,
            8 * total * count * channels,
            total * count * members * HEADS,
        )

    tiles = [tile_of(d, devices) for d in range(devices)]
    owner = {t: d for d, t in enumerate(tiles)}
    rightward = [(owner[t], owner[t + 1]) for t in range(devices - 1)]
    leftward = [(target, source) for source, target in rightward]

    def conv_tile(first, last, spans, parts):
        total = last - first
        operands = [p[k] for k in range(4) for p in parts]
        messages = (devices, total, block, channels)
        return call(
            functools.partial(conv_tile_kernel, 1, first, last, rows, spans, members),
            "conv_tile",
            (*operands, conv_weight, norm_gain, qkv_weight, out_weight, from_tile),
            [messages],
            [
                ((total + 2, count + 2 * members, channels), BF16),
                ((total, count, channels), BF16),
                (conv_shape, BF16),
            ]
            + attention_weights
            + [(messages, BF16)],
            2 * total * count * channels * (6 * channels + 2 * taps),
            8 * total * count * channels,
            total * count * members * HEADS,
        )[0]

    def place(first, last, arrived, earlier):
        total = last - first
        operands = [arrived, to_slab] + ([] if earlier is None else [earlier])
        return call(
            functools.partial(place_kernel, first),
            "place",
            operands,
            [(local, rows, cols, channels)],
            [(arrived.shape, BF16), square, ((local, total, cols, channels), BF16)],
            2 * total * count * count * channels,
            4 * total * count * channels,
            aliases={} if earlier is None else {2: 0},
        )[0]

    arrived = [exchange(conv_slab(*span)) for span in spans_in]
    parts = []
    result = None
    for rows_in in arrived:
        state, normed, low, high = attend(rows_in)
        from_left = lax.ppermute(high, "mem", rightward)
        from_right = lax.ppermute(low, "mem", leftward)
        parts.append((state, normed, from_left, from_right))
    returned = []
    for k, (first, last) in enumerate(spans_out):
        lo = 0 if k == 0 else k - 1
        messages = conv_tile(first, last, spans_in[lo : k + 1], parts[lo : k + 1])
        returned.append(exchange(messages))
    for span, arrival in zip(spans_out, returned):
        result = place(*span, arrival, result)
    return result


def solution(mesh):
    return jax.shard_map(
        body,
        mesh=mesh,
        in_specs=(P(("grp", "mem"), None, None, None), P(), P(), P(), P()),
        out_specs=P(("grp", "mem"), None, None, None),
        check_vma=False,
    )
```

```python
import functools

import jax
import jax.numpy as jnp
import numpy as np
from jax import lax
from jax.experimental import pallas as pl
from jax.experimental.pallas import tpu as pltpu
from jax.sharding import PartitionSpec as P

HEADS = 8
BLOCKS = 2
LANES = 128
epsilon = 1e-06
VMEM_LIMIT = 40 * 1024 * 1024
UNROLL = 4

F32 = jnp.float32
BF16 = jnp.bfloat16


def tile_of(device, count):
    if count % 4:
        return device
    group, inner = device // 4, device % 4
    if group % 2:
        inner = (2, 3, 0, 1)[inner]
    return group * 4 + inner


def one_hot(sources):
    matrix = np.zeros((len(sources), len(sources)), np.float32)
    matrix[np.arange(len(sources)), np.asarray(sources)] = 1.0
    return jnp.asarray(matrix, BF16)


def shuffles(count, local, cols):
    width = cols // count
    members = count * local
    tiles = [tile_of(d, count) for d in range(count)]
    to_message = [
        m * cols + tiles[d] * width + c
        for d in range(count)
        for m in range(local)
        for c in range(width)
    ]
    to_slab = np.argsort(to_message)
    to_tile = [
        d * local * width + m * width + c
        for c in range(width)
        for d in range(count)
        for m in range(local)
    ]
    from_tile = np.argsort(to_tile)
    return one_hot(to_message), one_hot(to_tile), one_hot(from_tile), one_hot(to_slab)


def normalize(widened, gain):
    inverse = lax.rsqrt(jnp.mean(widened * widened, axis=-1, keepdims=True) + epsilon)
    return widened * inverse * gain


def gated(conv_out, channels):
    return conv_out[:, :channels] * jax.nn.sigmoid(conv_out[:, channels:])


def shuffled(matrix, rows):
    return jnp.dot(matrix, rows, preferred_element_type=F32)


def groups_of(total, most=UNROLL):
    pieces = -(-total // most)
    edges = [total * k // pieces for k in range(pieces + 1)]
    return [(edges[k], edges[k + 1]) for k in range(pieces)]


def attention_rows(state, gain, wqv_t, wk, wout, members):
    total, channels = state.shape
    size = channels // HEADS
    group = LANES // size
    packed = LANES // members
    factor = float(np.log2(np.e) / np.sqrt(size))
    normed = normalize(state, gain).astype(BF16)
    keys = jnp.dot(normed, wk, preferred_element_type=F32).astype(BF16)
    qv_t = lax.dot_general(
        wqv_t, normed, (((1,), (1,)), ((), ())), preferred_element_type=F32
    ).astype(BF16)
    lane = lax.broadcasted_iota(jnp.int32, (members, LANES), 1)
    masks = [
        ((lane >= k * members) & (lane < (k + 1) * members)).astype(F32).astype(BF16)
        for k in range(packed)
    ]
    spans = [slice(j * LANES, (j + 1) * LANES) for j in range(total // LANES)]
    quads = range(channels // LANES)
    scores = {}
    for j, span in enumerate(spans):
        for q in quads:
            blocks = []
            for h in range(group):
                row = q * LANES + h * size
                parts = [jnp.zeros((size, LANES), BF16)] * group
                parts[h] = qv_t[row : row + size, span]
                blocks.append(jnp.concatenate(parts, axis=1))
            scores[j, q] = jnp.dot(
                keys[span, q * LANES : (q + 1) * LANES],
                jnp.concatenate(blocks, axis=0),
                preferred_element_type=F32,
            )
    weights = {}
    for j in range(len(spans)):
        for q in quads:
            for h in range(group):
                square = scores[j, q][:, h * LANES : (h + 1) * LANES]
                dense = square[:members]
                for k in range(1, packed):
                    dense = jnp.where(
                        lane < k * members, dense, square[k * members : (k + 1) * members]
                    )
                top = jnp.max(dense, axis=0, keepdims=True)
                expo = jnp.exp2((dense - top) * factor)
                inverse = 1.0 / jnp.sum(expo, axis=0, keepdims=True)
                spread = expo.astype(BF16)
                if packed > 1:
                    spread = jnp.concatenate([spread * mask for mask in masks], axis=0)
                weights[j, q, h] = spread, inverse
    columns = []
    for j, span in enumerate(spans):
        pieces = []
        for q in quads:
            for h in range(0, group, 2):
                row = channels + q * LANES + h * size
                mixed = jnp.dot(
                    qv_t[row : row + 2 * size, span],
                    jnp.concatenate([weights[j, q, h + k][0] for k in range(2)], axis=1),
                    preferred_element_type=F32,
                )
                for k in range(2):
                    own = mixed[k * size : (k + 1) * size, k * LANES : (k + 1) * LANES]
                    pieces.append((own * weights[j, q, h + k][1]).astype(BF16))
        columns.append(jnp.concatenate(pieces, axis=0))
    attended_t = jnp.concatenate(columns, axis=1)
    update = lax.dot_general(
        attended_t, wout, (((0,), (0,)), ((), ())), preferred_element_type=F32
    )
    return state + update


class Copies:
    def __init__(self, semaphores):
        self.semaphores = semaphores
        self.used = 0

    def start(self, source, target):
        copy = pltpu.make_async_copy(source, target, self.semaphores.at[self.used])
        self.used += 1
        copy.start()
        return copy


def wait_all(copies):
    for copy in copies:
        copy.wait()


def conv_slab_kernel(
    layer, first, last, staging, field_hbm, gain_hbm, weight_hbm, order_hbm, *refs,
):
    if staging:
        (qkv_hbm, wout_hbm, to_tile_hbm, from_tile_hbm, to_slab_hbm, out,
         later_gain, later_weight, wqv_t, wk, wout, to_tile, from_tile, to_slab,
         field, gain, weight, order, padded, qkv, semaphores) = refs
    else:
        out, field, gain, weight, order, padded, semaphores = refs
    local, rows, cols, channels = field_hbm.shape
    count = local * cols
    copies = Copies(semaphores)
    low = max(first - 1, 0)
    groups = groups_of(last - first)
    gain_copy = copies.start(gain_hbm, gain)
    fields, late, staged = [], [], []
    ready = low
    for k, (begin, end) in enumerate(groups):
        needed = min(first + end + 1, rows)
        part = slice(ready - low, needed - low)
        fields.append(copies.start(field_hbm.at[:, ready:needed], field.at[:, part]))
        ready = needed
        if k == 0:
            late.append(copies.start(weight_hbm.at[layer], weight))
            late.append(copies.start(order_hbm, order))
    if staging:
        staged = [
            copies.start(qkv_hbm, qkv),
            copies.start(gain_hbm, later_gain),
            copies.start(weight_hbm.at[layer + 1], later_weight),
            copies.start(wout_hbm, wout),
            copies.start(to_tile_hbm, to_tile),
            copies.start(from_tile_hbm, from_tile),
            copies.start(to_slab_hbm, to_slab),
        ]
    column = lax.broadcasted_iota(jnp.int32, (count, 1), 0) % cols
    zeros = jnp.zeros(padded.shape[1:], BF16)
    if first == 0:
        padded[0] = zeros
    if last == rows:
        padded[last - first + 1] = zeros
    gain_copy.wait()
    gain_row = gain[layer, 0:1]

    def prepare(row):
        widened = field[:, row - low].reshape(count, channels).astype(F32)
        normed = normalize(widened, gain_row)
        left = jnp.where(column == 0, 0.0, pltpu.roll(normed, 1, 0))
        right = jnp.where(column == cols - 1, 0.0, pltpu.roll(normed, count - 1, 0))
        slot = row - first + 1
        padded[slot, 0] = left.astype(BF16)
        padded[slot, 1] = normed.astype(BF16)
        padded[slot, 2] = right.astype(BF16)

    ready = low
    for k, (begin, end) in enumerate(groups):
        needed = min(first + end + 1, rows)
        fields[k].wait()
        for row in range(ready, needed):
            prepare(row)
        ready = needed
        if k == 0:
            wait_all(late)
        taps = [
            jnp.concatenate(
                [padded[i + di, dj] for di in range(3) for dj in range(3)], axis=1
            )
            for i in range(begin, end)
        ]
        conv_out = jnp.dot(
            jnp.concatenate(taps, axis=0),
            weight[...].reshape(9 * channels, 2 * channels),
            preferred_element_type=F32,
        )
        update = gated(conv_out, channels)
        for i in range(begin, end):
            widened = field[:, first + i - low].reshape(count, channels).astype(F32)
            part = update[(i - begin) * count : (i - begin + 1) * count]
            moved = shuffled(order[...], (widened + part).astype(BF16))
            out[:, i] = moved.reshape(out.shape[0], out.shape[2], channels).astype(BF16)
    if staging:
        wait_all(staged)
        for b in range(BLOCKS):
            wqv_t[b, :channels] = qkv[b, :, :channels].T
            wqv_t[b, channels:] = qkv[b, :, 2 * channels :].T
            wk[b] = qkv[b, :, channels : 2 * channels]


def attend_kernel(
    layer, members, arrived, gain, wqv_t, wk, wout, order, state, normed, low, high,
):
    total, count, channels = state.shape
    for begin, end in groups_of(total):
        joined = jnp.concatenate(
            [
                shuffled(order[...], arrived[:, i].reshape(count, channels))
                for i in range(begin, end)
            ],
            axis=0,
        )
        joined = attention_rows(
            joined, gain[layer, 1:2], wqv_t[layer], wk[layer], wout[layer], members
        ).astype(BF16)
        following = normalize(joined.astype(F32), gain[layer + 1, 0:1]).astype(BF16)
        for i in range(begin, end):
            span = slice((i - begin) * count, (i - begin + 1) * count)
            state[i] = joined[span]
            normed[i] = following[span]
            low[i] = following[span][:members]
            high[i] = following[span][count - members :]


def conv_tile_kernel(layer, first, last, rows, spans, members, cells, halo, *refs):
    pieces = len(spans)
    states, refs = refs[:pieces], refs[pieces:]
    normeds, refs = refs[:pieces], refs[pieces:]
    if halo:
        lows, refs = refs[:pieces], refs[pieces:]
        highs, refs = refs[:pieces], refs[pieces:]
        inner, order, refs = refs[0], refs[1], refs[2:]
    weight, gain, wqv_t, wk, wout, out = refs
    count, channels = states[0].shape[1:]
    total = last - first
    size = len(cells) * members
    zeros = jnp.zeros((members, channels), BF16)

    def piece_of(row):
        for k, (begin, end) in enumerate(spans):
            if begin <= row < end:
                return k, row - begin

    def tap(row, cell):
        if not 0 <= row < rows:
            return zeros
        k, place = piece_of(row)
        if cell < 0:
            return lows[k][place]
        if cell * members == count:
            return highs[k][place]
        return normeds[k][place, cell * members : (cell + 1) * members]

    def held(row, cell):
        k, place = piece_of(row)
        return states[k][place, cell * members : (cell + 1) * members]

    for begin, end in groups_of(total, UNROLL * count // size):
        taps = [
            jnp.concatenate(
                [
                    jnp.concatenate(
                        [tap(first + i + di - 1, cell + dj - 1) for cell in cells], axis=0
                    )
                    for di in range(3)
                    for dj in range(3)
                ],
                axis=1,
            )
            for i in range(begin, end)
        ]
        conv_out = jnp.dot(
            jnp.concatenate(taps, axis=0),
            weight[...].reshape(9 * channels, 2 * channels),
            preferred_element_type=F32,
        )
        joined = jnp.concatenate(
            [held(first + i, cell) for i in range(begin, end) for cell in cells], axis=0
        ).astype(F32)
        joined = (joined + gated(conv_out, channels)).astype(BF16).astype(F32)
        joined = attention_rows(
            joined, gain[layer, 1:2], wqv_t[layer], wk[layer], wout[layer], members
        ).astype(BF16)
        for i in range(begin, end):
            own = joined[(i - begin) * size : (i - begin + 1) * size]
            if halo:
                full = jnp.concatenate(
                    [own[:members], inner[i], own[members:]] if size < count else [own], axis=0
                )
                moved = shuffled(order[...], full)
                out[:, i] = moved.reshape(out.shape[0], out.shape[2], channels).astype(BF16)
            else:
                out[i] = own


def place_kernel(first, *refs):
    arrived, order, out_hbm, out, semaphores = refs[-5:]
    local, total, cols, channels = out.shape
    copies = Copies(semaphores)
    outputs = []
    for begin, end in groups_of(total, 2):
        for i in range(begin, end):
            moved = shuffled(order[...], arrived[:, i].reshape(local * cols, channels))
            out[:, i] = moved.reshape(local, cols, channels).astype(BF16)
        outputs.append(
            copies.start(out.at[:, begin:end], out_hbm.at[:, first + begin : first + end])
        )
    wait_all(outputs)


def call(kernel, name, far, near, outs, scratch, flops, moved, transcendentals=0, aliases=None):
    far = [pltpu.with_memory_space_constraint(x, pltpu.HBM) for x in far]
    near = [pltpu.with_memory_space_constraint(x, pltpu.VMEM) for x in near]
    anywhere, vmem = pl.BlockSpec(memory_space=pl.ANY), pl.BlockSpec(memory_space=pltpu.VMEM)
    scratch_shapes = [pltpu.VMEM(shape, dtype) for shape, dtype in scratch]
    if scratch:
        scratch_shapes.append(pltpu.SemaphoreType.DMA((32,)))
    return pl.pallas_call(
        kernel,
        out_shape=[
            pltpu.VMEM(shape, dtype) if is_near else jax.ShapeDtypeStruct(shape, dtype)
            for shape, dtype, is_near in outs
        ],
        in_specs=[anywhere] * len(far) + [vmem] * len(near),
        out_specs=[vmem if is_near else anywhere for _, _, is_near in outs],
        scratch_shapes=scratch_shapes,
        input_output_aliases=aliases or {},
        compiler_params=pltpu.CompilerParams(vmem_limit_bytes=VMEM_LIMIT),
        cost_estimate=pl.CostEstimate(
            flops=flops, bytes_accessed=moved, transcendentals=transcendentals
        ),
        name=name,
    )(*far, *near)


def body(field, norm_gain, conv_weight, qkv_weight, out_weight):
    local, rows, cols, channels = field.shape
    devices = lax.axis_size("mem")
    width = cols // devices
    members = devices * local
    count = local * cols
    block = local * width
    to_message, to_tile, from_tile, to_slab = shuffles(devices, local, cols)
    taps = conv_weight.shape[1] * conv_weight.shape[2] * channels
    conv_shape = conv_weight.shape[1:]

    split_in = rows // 2 + 1
    split_out = split_in - 1
    spans_in = ((0, split_in), (split_in, rows))
    spans_out = ((0, split_out), (split_out, rows))
    square = ((count, count), BF16)

    def conv_slab(first, last):
        total = last - first
        held = min(last + 1, rows) - max(first - 1, 0)
        staging = last == rows
        far = [field, norm_gain, conv_weight, to_message]
        outs = [((devices, total, block, channels), BF16, True)]
        scratch = [
            ((local, held, cols, channels), BF16),
            (norm_gain.shape, F32),
            (conv_shape, BF16),
            square,
            ((total + 2, 3, count, channels), BF16),
        ]
        if staging:
            far += [qkv_weight, out_weight, to_tile, from_tile, to_slab]
            outs += [
                (norm_gain.shape, F32, True),
                (conv_shape, BF16, True),
                ((BLOCKS, 2 * channels, channels), BF16, True),
                ((BLOCKS, channels, channels), BF16, True),
                (out_weight.shape, BF16, True),
            ] + [(*square, True)] * 3
            scratch.append((qkv_weight.shape, BF16))
        return call(
            functools.partial(conv_slab_kernel, 0, first, last, staging),
            "conv_slab",
            far,
            [],
            outs,
            scratch,
            2 * total * count * taps * 2 * channels,
            4 * total * count * channels,
            total * count * channels,
        )

    def exchange(messages):
        return lax.all_to_all(messages, "mem", split_axis=0, concat_axis=0, tiled=True)

    tiles = [tile_of(d, devices) for d in range(devices)]
    owner = {t: d for d, t in enumerate(tiles)}
    rightward = [(owner[t], owner[t + 1]) for t in range(devices - 1)]
    leftward = [(target, source) for source, target in rightward]

    arrived = []
    for span in spans_in:
        messages, *staged = conv_slab(*span)
        arrived.append(exchange(messages))
    gain, later_weight, wqv_t, wk, wout, to_tile, from_tile, to_slab = staged

    def attend(arrival):
        total = arrival.shape[1]
        whole, edge = (total, count, channels), (total, members, channels)
        return call(
            functools.partial(attend_kernel, 0, members),
            "attend",
            [],
            [arrival, gain, wqv_t, wk, wout, to_tile],
            [(shape, BF16, True) for shape in (whole, whole, edge, edge)],
            [],
            2 * total * count * channels * 6 * channels,
            8 * total * count * channels,
            total * count * members * HEADS,
        )

    def conv_tile(first, last, spans, parts, inner):
        total = last - first
        halo = inner is not None
        cells = (0, width - 1) if halo else tuple(range(1, width - 1))
        if not cells:
            return jnp.zeros((1, members, channels), BF16)
        operands = [p[k] for k in range(4 if halo else 2) for p in parts]
        if halo:
            operands += [inner, from_tile]
        size = len(cells) * members
        shape = (devices, total, block, channels) if halo else (total, size, channels)
        return call(
            functools.partial(
                conv_tile_kernel, 1, first, last, rows, spans, members, cells, halo
            ),
            "conv_edges" if halo else "conv_inner",
            [],
            [*operands, later_weight, gain, wqv_t, wk, wout],
            [(shape, BF16, True)],
            [],
            2 * total * size * channels * (6 * channels + 2 * taps),
            8 * total * count * channels,
            total * size * members * HEADS,
        )[0]

    def place(first, last, arrival, earlier):
        total = last - first
        return call(
            functools.partial(place_kernel, first),
            "place",
            [] if earlier is None else [earlier],
            [arrival, to_slab],
            [((local, rows, cols, channels), BF16, False)],
            [((local, total, cols, channels), BF16)],
            2 * total * count * count * channels,
            4 * total * count * channels,
            aliases={} if earlier is None else {0: 0},
        )[0]

    parts = []
    for arrival in arrived:
        state, normed, low, high = attend(arrival)
        from_left = lax.ppermute(high, "mem", rightward)
        from_right = lax.ppermute(low, "mem", leftward)
        parts.append((state, normed, from_left, from_right))
    returned = []
    for k, (first, last) in enumerate(spans_out):
        lo = 0 if k == 0 else k - 1
        spans = spans_in[lo : k + 1]
        inner = conv_tile(first, last, spans, parts[lo : k + 1], None)
        messages = conv_tile(first, last, spans, parts[lo : k + 1], inner)
        returned.append(exchange(messages))
    result = None
    for span, arrival in zip(spans_out, returned):
        result = place(*span, arrival, result)
    return result


def solution(mesh):
    return jax.shard_map(
        body,
        mesh=mesh,
        in_specs=(P(("grp", "mem"), None, None, None), P(), P(), P(), P()),
        out_specs=P(("grp", "mem"), None, None, None),
        check_vma=False,
    )
```

```python
import functools

import jax
import jax.numpy as jnp
import numpy as np
from jax import lax
from jax.experimental import pallas as pl
from jax.experimental.pallas import tpu as pltpu
from jax.sharding import PartitionSpec as P

HEADS = 8
BLOCKS = 2
LANES = 128
epsilon = 1e-06
VMEM_LIMIT = 40 * 1024 * 1024
UNROLL = 4
CUTS = (7,)
AHEAD = 0
SPLIT_TILE = True
WQ_T, WV_T, WK, WOUT, ORDER, FINAL = range(6)

F32 = jnp.float32
BF16 = jnp.bfloat16


def tile_of(device, count):
    if count % 4:
        return device
    group, inner = device // 4, device % 4
    if group % 2:
        inner = (2, 3, 0, 1)[inner]
    return group * 4 + inner


def one_hot(sources):
    matrix = np.zeros((len(sources), len(sources)), np.float32)
    matrix[np.arange(len(sources)), np.asarray(sources)] = 1.0
    return jnp.asarray(matrix, BF16)


def shuffles(count, local, cols):
    width = cols // count
    members = count * local
    tiles = [tile_of(d, count) for d in range(count)]
    to_message = [
        m * cols + tiles[d] * width + c
        for d in range(count)
        for m in range(local)
        for c in range(width)
    ]
    to_slab = np.argsort(to_message)
    to_tile = [
        d * local * width + m * width + c
        for c in range(width)
        for d in range(count)
        for m in range(local)
    ]
    from_tile = np.argsort(to_tile)
    return one_hot(to_message), one_hot(to_tile), one_hot(from_tile), one_hot(to_slab)


def normalize(widened, gain):
    inverse = lax.rsqrt(jnp.mean(widened * widened, axis=-1, keepdims=True) + epsilon)
    return widened * inverse * gain


def gated(conv_out, channels):
    return conv_out[:, :channels] * jax.nn.sigmoid(conv_out[:, channels:])


def shuffled(matrix, rows):
    return jnp.dot(matrix, rows, preferred_element_type=F32)


def groups_of(total, most=UNROLL):
    pieces = -(-total // most)
    edges = [total * k // pieces for k in range(pieces + 1)]
    return [(edges[k], edges[k + 1]) for k in range(pieces)]


def attention_rows(state, gain, squares, members):
    total, channels = state.shape
    size = channels // HEADS
    group = LANES // size
    packed = LANES // members
    factor = float(np.log2(np.e) / np.sqrt(size))
    normed = normalize(state, gain).astype(BF16)
    keys = jnp.dot(normed, squares[WK], preferred_element_type=F32).astype(BF16)
    wqv_t = squares[WQ_T : WV_T + 1].reshape(2 * channels, channels)
    qv_t = lax.dot_general(
        wqv_t, normed, (((1,), (1,)), ((), ())), preferred_element_type=F32
    ).astype(BF16)
    lane = lax.broadcasted_iota(jnp.int32, (members, LANES), 1)
    masks = [
        ((lane >= k * members) & (lane < (k + 1) * members)).astype(F32).astype(BF16)
        for k in range(packed)
    ]
    spans = [slice(j * LANES, (j + 1) * LANES) for j in range(total // LANES)]
    quads = range(channels // LANES)
    scores = {}
    for j, span in enumerate(spans):
        for q in quads:
            blocks = []
            for h in range(group):
                row = q * LANES + h * size
                parts = [jnp.zeros((size, LANES), BF16)] * group
                parts[h] = qv_t[row : row + size, span]
                blocks.append(jnp.concatenate(parts, axis=1))
            scores[j, q] = jnp.dot(
                keys[span, q * LANES : (q + 1) * LANES],
                jnp.concatenate(blocks, axis=0),
                preferred_element_type=F32,
            )
    weights = {}
    for j in range(len(spans)):
        for q in quads:
            for h in range(group):
                square = scores[j, q][:, h * LANES : (h + 1) * LANES]
                dense = square[:members]
                for k in range(1, packed):
                    dense = jnp.where(
                        lane < k * members, dense, square[k * members : (k + 1) * members]
                    )
                top = jnp.max(dense, axis=0, keepdims=True)
                expo = jnp.exp2((dense - top) * factor)
                inverse = 1.0 / jnp.sum(expo, axis=0, keepdims=True)
                spread = expo.astype(BF16)
                if packed > 1:
                    spread = jnp.concatenate([spread * mask for mask in masks], axis=0)
                weights[j, q, h] = spread, inverse
    columns = []
    for j, span in enumerate(spans):
        pieces = []
        for q in quads:
            for h in range(0, group, 2):
                row = channels + q * LANES + h * size
                mixed = jnp.dot(
                    qv_t[row : row + 2 * size, span],
                    jnp.concatenate([weights[j, q, h + k][0] for k in range(2)], axis=1),
                    preferred_element_type=F32,
                )
                for k in range(2):
                    own = mixed[k * size : (k + 1) * size, k * LANES : (k + 1) * LANES]
                    pieces.append((own * weights[j, q, h + k][1]).astype(BF16))
        columns.append(jnp.concatenate(pieces, axis=0))
    attended_t = jnp.concatenate(columns, axis=1)
    update = lax.dot_general(
        attended_t, squares[WOUT], (((0,), (0,)), ((), ())), preferred_element_type=F32
    )
    return state + update


class Copies:
    def __init__(self, semaphores):
        self.semaphores = semaphores
        self.used = 0

    def start(self, source, target):
        copy = pltpu.make_async_copy(source, target, self.semaphores.at[self.used])
        self.used += 1
        copy.start()
        return copy


def wait_all(copies):
    for copy in copies:
        copy.wait()


def conv_slab_kernel(
    layer, first, last, staging, field_hbm, gain_hbm, weight_hbm, order_hbm, *refs,
):
    if staging:
        (qkv_hbm, wout_hbm, to_tile_hbm, from_tile_hbm, to_slab_hbm, out_hbm,
         later_gain, later_weight, stacks,
         field, gain, weight, order, padded, out, qkv, semaphores) = refs
    else:
        out_hbm, field, gain, weight, order, padded, out, semaphores = refs
    local, rows, cols, channels = field_hbm.shape
    count = local * cols
    copies = Copies(semaphores)
    low = max(first - 1, 0)
    groups = groups_of(last - first)
    gain_copy = copies.start(gain_hbm, gain)
    fields, late, staged = [], [], []
    ready = low
    for k, (begin, end) in enumerate(groups):
        needed = min(first + end + 1, rows)
        part = slice(ready - low, needed - low)
        fields.append(copies.start(field_hbm.at[:, ready:needed], field.at[:, part]))
        ready = needed
        if k == 0:
            late = [copies.start(weight_hbm.at[layer, di], weight.at[di]) for di in range(3)]
            order_copy = copies.start(order_hbm, order)
    if staging:
        staged = [
            copies.start(qkv_hbm, qkv),
            copies.start(gain_hbm, later_gain),
            copies.start(weight_hbm.at[layer + 1], later_weight),
            copies.start(wout_hbm.at[0], stacks.at[0, WOUT]),
            copies.start(wout_hbm.at[1], stacks.at[1, WOUT]),
            copies.start(to_tile_hbm, stacks.at[0, ORDER]),
            copies.start(from_tile_hbm, stacks.at[1, ORDER]),
            copies.start(to_slab_hbm, stacks.at[0, FINAL]),
        ]
    column = lax.broadcasted_iota(jnp.int32, (count, 1), 0) % cols
    zeros = jnp.zeros(padded.shape[1:], BF16)
    if first == 0:
        padded[0] = zeros
    if last == rows:
        padded[last - first + 1] = zeros
    gain_copy.wait()
    gain_row = gain[layer, 0:1]

    def prepare(row):
        widened = field[:, row - low].reshape(count, channels).astype(F32)
        normed = normalize(widened, gain_row)
        left = jnp.where(column == 0, 0.0, pltpu.roll(normed, 1, 0))
        right = jnp.where(column == cols - 1, 0.0, pltpu.roll(normed, count - 1, 0))
        slot = row - first + 1
        padded[slot, 0] = left.astype(BF16)
        padded[slot, 1] = normed.astype(BF16)
        padded[slot, 2] = right.astype(BF16)

    ready = low
    outputs = []
    for k, (begin, end) in enumerate(groups):
        needed = min(first + end + 1, rows)
        fields[k].wait()
        for row in range(ready, needed):
            prepare(row)
        ready = needed
        taps = [
            jnp.concatenate(
                [
                    jnp.concatenate([padded[i + di, dj] for dj in range(3)], axis=1)
                    for i in range(begin, end)
                ],
                axis=0,
            )
            for di in range(3)
        ]
        if k == 0:
            conv_out = 0.0
            for di in range(3):
                late[di].wait()
                conv_out += jnp.dot(
                    taps[di],
                    weight[di].reshape(3 * channels, 2 * channels),
                    preferred_element_type=F32,
                )
            order_copy.wait()
        else:
            conv_out = jnp.dot(
                jnp.concatenate(taps, axis=1),
                weight[...].reshape(9 * channels, 2 * channels),
                preferred_element_type=F32,
            )
        update = gated(conv_out, channels)
        for i in range(begin, end):
            widened = field[:, first + i - low].reshape(count, channels).astype(F32)
            part = update[(i - begin) * count : (i - begin + 1) * count]
            moved = shuffled(order[...], (widened + part).astype(BF16))
            out[:, i] = moved.reshape(out.shape[0], out.shape[2], channels).astype(BF16)
        outputs.append(copies.start(out.at[:, begin:end], out_hbm.at[:, begin:end]))
    if staging:
        wait_all(staged)
        for b in range(BLOCKS):
            stacks[b, WQ_T] = qkv[b, :, :channels].T
            stacks[b, WV_T] = qkv[b, :, 2 * channels :].T
            stacks[b, WK] = qkv[b, :, channels : 2 * channels]
    wait_all(outputs)


def attend_kernel(
    layer, members, arrived, gain, stacks, state, normed, low, high, *local_copy,
):
    total, count, channels = state.shape
    squares = stacks.at[layer]
    if local_copy:
        copy = pltpu.make_async_copy(arrived, local_copy[0], local_copy[1].at[0])
        copy.start()
        copy.wait()
        arrived = local_copy[0]
    for begin, end in groups_of(total):
        joined = jnp.concatenate(
            [
                shuffled(squares[ORDER], arrived[:, i].reshape(count, channels))
                for i in range(begin, end)
            ],
            axis=0,
        )
        joined = attention_rows(
            joined, gain[layer, 1:2], squares, members
        ).astype(BF16)
        following = normalize(joined.astype(F32), gain[layer + 1, 0:1]).astype(BF16)
        for i in range(begin, end):
            span = slice((i - begin) * count, (i - begin + 1) * count)
            state[i] = joined[span]
            normed[i] = following[span]
            low[i] = following[span][:members]
            high[i] = following[span][count - members :]


def conv_tile_kernel(layer, first, last, rows, spans, members, cells, halo, *refs):
    pieces = len(spans)
    states, refs = refs[:pieces], refs[pieces:]
    normeds, refs = refs[:pieces], refs[pieces:]
    if halo:
        lows, refs = refs[:pieces], refs[pieces:]
        highs, refs = refs[:pieces], refs[pieces:]
        if len(cells) * members < states[0].shape[1]:
            inner, partial, refs = *refs[:2], refs[2:]
    if halo:
        gain, stacks, weight, out_hbm, out, semaphores = refs
        copies = Copies(semaphores)
    else:
        gain, stacks, weight, out, partial = refs
    squares = stacks.at[layer]
    end_cell = states[0].shape[1] // members - 1
    outputs = []
    count, channels = states[0].shape[1:]
    total = last - first
    size = len(cells) * members
    zeros = jnp.zeros((members, channels), BF16)

    def piece_of(row):
        for k, (begin, end) in enumerate(spans):
            if begin <= row < end:
                return k, row - begin

    def tap(row, cell):
        if not 0 <= row < rows:
            return zeros
        k, place = piece_of(row)
        if cell < 0:
            return lows[k][place]
        if cell * members == count:
            return highs[k][place]
        return normeds[k][place, cell * members : (cell + 1) * members]

    def held(row, cell):
        k, place = piece_of(row)
        return states[k][place, cell * members : (cell + 1) * members]

    def conv(begin, end, cells, sides):
        taps = [
            jnp.concatenate(
                [
                    jnp.concatenate(
                        [tap(first + i + di - 1, cell + dj - 1) for cell in cells], axis=0
                    )
                    for di in range(3)
                    for dj in sides
                ],
                axis=1,
            )
            for i in range(begin, end)
        ]
        return jnp.dot(
            jnp.concatenate(taps, axis=0),
            weight[:, sides.start : sides.stop].reshape(3 * len(sides) * channels, 2 * channels),
            preferred_element_type=F32,
        )

    for begin, end in groups_of(total, UNROLL * count // size):
        run = end - begin
        if not halo or size == count:
            conv_out = conv(begin, end, cells, range(3))
        else:
            beside = [
                conv(begin, end, cells[:1], range(1)).reshape(run, members, 2 * channels),
                conv(begin, end, cells[1:], range(2, 3)).reshape(run, members, 2 * channels),
            ]
            conv_out = jnp.concatenate(beside, axis=1) + partial[begin:end]
            conv_out = conv_out.reshape(run * size, 2 * channels)
        if not halo:
            own = conv(begin, end, (0,), range(1, 3))
            partial[begin:end, :members] = own.reshape(run, members, 2 * channels)
            own = conv(begin, end, (end_cell,), range(2))
            partial[begin:end, members:] = own.reshape(run, members, 2 * channels)
        joined = jnp.concatenate(
            [held(first + i, cell) for i in range(begin, end) for cell in cells], axis=0
        ).astype(F32)
        joined = (joined + gated(conv_out, channels)).astype(BF16).astype(F32)
        joined = attention_rows(
            joined, gain[layer, 1:2], squares, members
        ).astype(BF16)
        for i in range(begin, end):
            own = joined[(i - begin) * size : (i - begin + 1) * size]
            if halo:
                full = jnp.concatenate(
                    [own[:members], inner[i], own[members:]] if size < count else [own], axis=0
                )
                moved = shuffled(squares[ORDER], full)
                out[:, i] = moved.reshape(out.shape[0], out.shape[2], channels).astype(BF16)
            else:
                out[i] = own
        if halo:
            outputs.append(copies.start(out.at[:, begin:end], out_hbm.at[:, begin:end]))
    wait_all(outputs)


def place_kernel(first, earlier, *refs):
    if earlier:
        arrived, stacks, out_hbm, out, semaphores = refs[-5:]
    else:
        arrived_hbm, stacks, out_hbm, arrived, out, semaphores = refs
        copy = pltpu.make_async_copy(arrived_hbm, arrived, semaphores.at[31])
        copy.start()
        copy.wait()
    local, total, cols, channels = out.shape
    copies = Copies(semaphores)
    outputs = []
    for begin, end in groups_of(total, 2):
        for i in range(begin, end):
            moved = shuffled(stacks[0, FINAL], arrived[:, i].reshape(local * cols, channels))
            out[:, i] = moved.reshape(local, cols, channels).astype(BF16)
        outputs.append(
            copies.start(out.at[:, begin:end], out_hbm.at[:, first + begin : first + end])
        )
    wait_all(outputs)


def call(
    kernel, name, far, near, outs, scratch, flops, moved, transcendentals=0, aliases=None
):
    far = [pltpu.with_memory_space_constraint(x, pltpu.HBM) for x in far]
    near = [pltpu.with_memory_space_constraint(x, pltpu.VMEM) for x in near]
    anywhere, vmem = pl.BlockSpec(memory_space=pl.ANY), pl.BlockSpec(memory_space=pltpu.VMEM)
    scratch_shapes = [pltpu.VMEM(shape, dtype) for shape, dtype in scratch]
    if scratch:
        scratch_shapes.append(pltpu.SemaphoreType.DMA((32,)))
    return pl.pallas_call(
        kernel,
        out_shape=[
            (pltpu.VMEM if is_near else pltpu.HBM)(shape, dtype)
            for shape, dtype, is_near in outs
        ],
        in_specs=[anywhere] * len(far) + [vmem] * len(near),
        out_specs=[vmem if is_near else anywhere for _, _, is_near in outs],
        scratch_shapes=scratch_shapes,
        input_output_aliases=aliases or {},
        compiler_params=pltpu.CompilerParams(vmem_limit_bytes=VMEM_LIMIT),
        cost_estimate=pl.CostEstimate(
            flops=flops, bytes_accessed=moved, transcendentals=transcendentals
        ),
        name=name,
    )(*far, *near)


def chunks(rows):
    edges = [0, *(round(rows * cut / 16) for cut in CUTS), rows]
    inner = [edge - 1 for edge in edges[1:-1]]
    outer = [0, *inner, rows]
    return tuple(zip(edges, edges[1:])), tuple(zip(outer, outer[1:]))


def body(field, norm_gain, conv_weight, qkv_weight, out_weight):
    local, rows, cols, channels = field.shape
    devices = lax.axis_size("mem")
    width = cols // devices
    members = devices * local
    count = local * cols
    block = local * width
    to_message, to_tile, from_tile, to_slab = shuffles(devices, local, cols)
    taps = conv_weight.shape[1] * conv_weight.shape[2] * channels
    conv_shape = conv_weight.shape[1:]

    spans_in, spans_out = chunks(rows)
    square = ((count, count), BF16)

    def conv_slab(first, last):
        total = last - first
        held = min(last + 1, rows) - max(first - 1, 0)
        staging = last == rows
        far = [field, norm_gain, conv_weight, to_message]
        messages = (devices, total, block, channels)
        outs = [(messages, BF16, False)]
        scratch = [
            ((local, held, cols, channels), BF16),
            (norm_gain.shape, F32),
            (conv_shape, BF16),
            square,
            ((total + 2, 3, count, channels), BF16),
            (messages, BF16),
        ]
        if staging:
            far += [qkv_weight, out_weight, to_tile, from_tile, to_slab]
            outs += [
                (norm_gain.shape, F32, True),
                (conv_shape, BF16, True),
                ((BLOCKS, 6, channels, channels), BF16, True),
            ]
            scratch.append((qkv_weight.shape, BF16))
        return call(
            functools.partial(conv_slab_kernel, 0, first, last, staging),
            "conv_slab",
            far,
            [],
            outs,
            scratch,
            2 * total * count * taps * 2 * channels,
            4 * total * count * channels,
            total * count * channels,
        )

    def exchange(messages):
        return lax.all_to_all(messages, "mem", split_axis=0, concat_axis=0, tiled=True)

    tiles = [tile_of(d, devices) for d in range(devices)]
    owner = {t: d for d, t in enumerate(tiles)}
    rightward = [(owner[t], owner[t + 1]) for t in range(devices - 1)]
    leftward = [(target, source) for source, target in rightward]

    arrived = []
    for span in spans_in:
        messages, *staged = conv_slab(*span)
        arrived.append(exchange(messages))
    gain, later_weight, stacks = staged

    def attend(arrival, is_far):
        total = arrival.shape[1]
        whole, edge = (total, count, channels), (total, members, channels)
        return call(
            functools.partial(attend_kernel, 0, members),
            "attend",
            [arrival] if is_far else [],
            [gain, stacks] if is_far else [arrival, gain, stacks],
            [(shape, BF16, True) for shape in (whole, whole, edge, edge)],
            [(arrival.shape, BF16)] if is_far else [],
            2 * total * count * channels * 6 * channels,
            8 * total * count * channels,
            total * count * members * HEADS,
        )

    def conv_tile(first, last, spans, parts, cells, halo, inner=()):
        total = last - first
        operands = [p[k] for k in range(4 if halo else 2) for p in parts]
        operands += inner
        size = len(cells) * members
        shape = (devices, total, block, channels) if halo else (total, size, channels)
        return call(
            functools.partial(
                conv_tile_kernel, 1, first, last, rows, spans, members, cells, halo
            ),
            "conv_edges" if halo else "conv_inner",
            [],
            [*operands, gain, stacks, later_weight],
            [(shape, BF16, not halo)]
            + ([] if halo else [((total, 2 * members, 2 * channels), F32, True)]),
            [(shape, BF16)] if halo else [],
            2 * total * size * channels * (6 * channels + 2 * taps),
            8 * total * count * channels,
            total * size * members * HEADS,
        )

    def place(first, last, arrival, earlier):
        total = last - first
        return call(
            functools.partial(place_kernel, first, earlier is not None),
            "place",
            [arrival] if earlier is None else [earlier],
            [stacks] if earlier is None else [arrival, stacks],
            [((local, rows, cols, channels), BF16, False)],
            ([(arrival.shape, BF16)] if earlier is None else [])
            + [((local, total, cols, channels), BF16)],
            2 * total * count * count * channels,
            4 * total * count * channels,
            aliases={} if earlier is None else {0: 0},
        )[0]

    parts, returned = [], []

    def attend_chunk(k):
        state, normed, low, high = attend(arrived[k], k == 0)
        from_left = lax.ppermute(high, "mem", rightward)
        from_right = lax.ppermute(low, "mem", leftward)
        parts.append((state, normed, from_left, from_right))

    def tile_chunk(k):
        lo = max(k - 1, 0)
        rest = (*spans_out[k], spans_in[lo : k + 1], parts[lo : k + 1])
        if SPLIT_TILE and width > 2:
            inner = conv_tile(*rest, tuple(range(1, width - 1)), False)
            (messages,) = conv_tile(*rest, (0, width - 1), True, inner)
        else:
            (messages,) = conv_tile(*rest, tuple(range(width)), True)
        returned.append(exchange(messages))

    for k in range(len(spans_in) + AHEAD):
        if k < len(spans_in):
            attend_chunk(k)
        if k >= AHEAD:
            tile_chunk(k - AHEAD)
    result = None
    for span, arrival in zip(spans_out, returned):
        result = place(*span, arrival, result)
    return result


def solution(mesh):
    return jax.shard_map(
        body,
        mesh=mesh,
        in_specs=(P(("grp", "mem"), None, None, None), P(), P(), P(), P()),
        out_specs=P(("grp", "mem"), None, None, None),
        check_vma=False,
    )
```

```python
import functools

import jax
import jax.numpy as jnp
import numpy as np
from jax import lax
from jax.experimental import pallas as pl
from jax.experimental.pallas import tpu as pltpu
from jax.sharding import PartitionSpec as P

HEADS = 8
BLOCKS = 2
LANES = 128
epsilon = 1e-06
VMEM_LIMIT = 40 * 1024 * 1024
UNROLL = 5
CUTS = (7,)
AHEAD = 0
SPLIT_TILE = True
WQ_T, WV_T, WK, WOUT, ORDER, FINAL = range(6)

F32 = jnp.float32
BF16 = jnp.bfloat16


def tile_of(device, count):
    if count % 4:
        return device
    group, inner = device // 4, device % 4
    if group % 2:
        inner = (2, 3, 0, 1)[inner]
    return group * 4 + inner


def one_hot(sources):
    matrix = np.zeros((len(sources), len(sources)), np.float32)
    matrix[np.arange(len(sources)), np.asarray(sources)] = 1.0
    return jnp.asarray(matrix, BF16)


def shuffles(count, local, cols):
    width = cols // count
    members = count * local
    tiles = [tile_of(d, count) for d in range(count)]
    to_message = [
        m * cols + tiles[d] * width + c
        for d in range(count)
        for m in range(local)
        for c in range(width)
    ]
    to_slab = np.argsort(to_message)
    to_tile = [
        d * local * width + m * width + c
        for c in range(width)
        for d in range(count)
        for m in range(local)
    ]
    from_tile = np.argsort(to_tile)
    return one_hot(to_message), one_hot(to_tile), one_hot(from_tile), one_hot(to_slab)


def normalize(widened, gain):
    inverse = lax.rsqrt(jnp.mean(widened * widened, axis=-1, keepdims=True) + epsilon)
    return widened * inverse * gain


def gated(conv_out, channels):
    return conv_out[:, :channels] * jax.nn.sigmoid(conv_out[:, channels:])


def shuffled(matrix, rows):
    return jnp.dot(matrix, rows, preferred_element_type=F32)


def groups_of(total, most=UNROLL):
    pieces = -(-total // most)
    edges = [total * k // pieces for k in range(pieces + 1)]
    return [(edges[k], edges[k + 1]) for k in range(pieces)]


def attention_rows(state, gain, squares, members):
    total, channels = state.shape
    size = channels // HEADS
    group = LANES // size
    packed = LANES // members
    factor = float(np.log2(np.e) / np.sqrt(size))
    normed = normalize(state, gain).astype(BF16)
    keys = jnp.dot(normed, squares[WK], preferred_element_type=F32).astype(BF16)
    wqv_t = squares[WQ_T : WV_T + 1].reshape(2 * channels, channels)
    qv_t = lax.dot_general(
        wqv_t, normed, (((1,), (1,)), ((), ())), preferred_element_type=F32
    ).astype(BF16)
    lane = lax.broadcasted_iota(jnp.int32, (members, LANES), 1)
    masks = [
        ((lane >= k * members) & (lane < (k + 1) * members)).astype(F32).astype(BF16)
        for k in range(packed)
    ]
    spans = [slice(j * LANES, (j + 1) * LANES) for j in range(total // LANES)]
    quads = range(channels // LANES)
    scores = {}
    for j, span in enumerate(spans):
        for q in quads:
            blocks = []
            for h in range(group):
                row = q * LANES + h * size
                parts = [jnp.zeros((size, LANES), BF16)] * group
                parts[h] = qv_t[row : row + size, span]
                blocks.append(jnp.concatenate(parts, axis=1))
            scores[j, q] = jnp.dot(
                keys[span, q * LANES : (q + 1) * LANES],
                jnp.concatenate(blocks, axis=0),
                preferred_element_type=F32,
            )
    weights = {}
    for j in range(len(spans)):
        for q in quads:
            for h in range(group):
                square = scores[j, q][:, h * LANES : (h + 1) * LANES]
                dense = square[:members]
                for k in range(1, packed):
                    dense = jnp.where(
                        lane < k * members, dense, square[k * members : (k + 1) * members]
                    )
                top = jnp.max(dense, axis=0, keepdims=True)
                expo = jnp.exp2((dense - top) * factor)
                inverse = 1.0 / jnp.sum(expo, axis=0, keepdims=True)
                spread = expo.astype(BF16)
                if packed > 1:
                    spread = jnp.concatenate([spread * mask for mask in masks], axis=0)
                weights[j, q, h] = spread, inverse
    columns = []
    for j, span in enumerate(spans):
        pieces = []
        for q in quads:
            for h in range(0, group, 2):
                row = channels + q * LANES + h * size
                mixed = jnp.dot(
                    qv_t[row : row + 2 * size, span],
                    jnp.concatenate([weights[j, q, h + k][0] for k in range(2)], axis=1),
                    preferred_element_type=F32,
                )
                for k in range(2):
                    own = mixed[k * size : (k + 1) * size, k * LANES : (k + 1) * LANES]
                    pieces.append((own * weights[j, q, h + k][1]).astype(BF16))
        columns.append(jnp.concatenate(pieces, axis=0))
    attended_t = jnp.concatenate(columns, axis=1)
    update = lax.dot_general(
        attended_t, squares[WOUT], (((0,), (0,)), ((), ())), preferred_element_type=F32
    )
    return state + update


class Copies:
    def __init__(self, semaphores):
        self.semaphores = semaphores
        self.used = 0

    def start(self, source, target):
        copy = pltpu.make_async_copy(source, target, self.semaphores.at[self.used])
        self.used += 1
        copy.start()
        return copy


def wait_all(copies):
    for copy in copies:
        copy.wait()


def conv_slab_kernel(
    layer, first, last, staging, field_hbm, gain_hbm, weight_hbm, order_hbm, *refs,
):
    if staging:
        (qkv_hbm, wout_hbm, to_tile_hbm, from_tile_hbm, to_slab_hbm, out_hbm,
         later_gain, later_weight, stacks,
         field, gain, weight, order, padded, out, qkv, semaphores) = refs
    else:
        out_hbm, field, gain, weight, order, padded, out, semaphores = refs
    local, rows, cols, channels = field_hbm.shape
    count = local * cols
    copies = Copies(semaphores)
    low = max(first - 1, 0)
    groups = groups_of(last - first)
    gain_copy = copies.start(gain_hbm, gain)
    fields, late, staged = [], [], []
    ready = low
    for k, (begin, end) in enumerate(groups):
        needed = min(first + end + 1, rows)
        part = slice(ready - low, needed - low)
        fields.append(copies.start(field_hbm.at[:, ready:needed], field.at[:, part]))
        ready = needed
        if k == 0:
            late = [copies.start(weight_hbm.at[layer, di], weight.at[di]) for di in range(3)]
            order_copy = copies.start(order_hbm, order)
    if staging:
        staged = [
            copies.start(qkv_hbm, qkv),
            copies.start(gain_hbm, later_gain),
            copies.start(weight_hbm.at[layer + 1], later_weight),
            copies.start(wout_hbm.at[0], stacks.at[0, WOUT]),
            copies.start(wout_hbm.at[1], stacks.at[1, WOUT]),
            copies.start(to_tile_hbm, stacks.at[0, ORDER]),
            copies.start(from_tile_hbm, stacks.at[1, ORDER]),
            copies.start(to_slab_hbm, stacks.at[0, FINAL]),
        ]
    column = lax.broadcasted_iota(jnp.int32, (count, 1), 0) % cols
    zeros = jnp.zeros(padded.shape[1:], BF16)
    if first == 0:
        padded[0] = zeros
    if last == rows:
        padded[last - first + 1] = zeros
    gain_copy.wait()
    gain_row = gain[layer, 0:1]

    def prepare(row):
        widened = field[:, row - low].reshape(count, channels).astype(F32)
        normed = normalize(widened, gain_row)
        left = jnp.where(column == 0, 0.0, pltpu.roll(normed, 1, 0))
        right = jnp.where(column == cols - 1, 0.0, pltpu.roll(normed, count - 1, 0))
        slot = row - first + 1
        padded[slot, 0] = left.astype(BF16)
        padded[slot, 1] = normed.astype(BF16)
        padded[slot, 2] = right.astype(BF16)

    ready = low
    outputs = []
    for k, (begin, end) in enumerate(groups):
        needed = min(first + end + 1, rows)
        fields[k].wait()
        for row in range(ready, needed):
            prepare(row)
        ready = needed
        taps = [
            jnp.concatenate(
                [
                    jnp.concatenate([padded[i + di, dj] for dj in range(3)], axis=1)
                    for i in range(begin, end)
                ],
                axis=0,
            )
            for di in range(3)
        ]
        if k == 0:
            conv_out = 0.0
            for di in range(3):
                late[di].wait()
                conv_out += jnp.dot(
                    taps[di],
                    weight[di].reshape(3 * channels, 2 * channels),
                    preferred_element_type=F32,
                )
            order_copy.wait()
        else:
            conv_out = jnp.dot(
                jnp.concatenate(taps, axis=1),
                weight[...].reshape(9 * channels, 2 * channels),
                preferred_element_type=F32,
            )
        update = gated(conv_out, channels)
        for i in range(begin, end):
            widened = field[:, first + i - low].reshape(count, channels).astype(F32)
            part = update[(i - begin) * count : (i - begin + 1) * count]
            moved = shuffled(order[...], (widened + part).astype(BF16))
            out[:, i] = moved.reshape(out.shape[0], out.shape[2], channels).astype(BF16)
        outputs.append(copies.start(out.at[:, begin:end], out_hbm.at[:, begin:end]))
    if staging:
        wait_all(staged)
        for b in range(BLOCKS):
            stacks[b, WQ_T] = qkv[b, :, :channels].T
            stacks[b, WV_T] = qkv[b, :, 2 * channels :].T
            stacks[b, WK] = qkv[b, :, channels : 2 * channels]
    wait_all(outputs)


def attend_kernel(
    layer, members, arrived, gain, stacks, state, normed, low, high, *local_copy,
):
    total, count, channels = state.shape
    squares = stacks.at[layer]
    if local_copy:
        copy = pltpu.make_async_copy(arrived, local_copy[0], local_copy[1].at[0])
        copy.start()
        copy.wait()
        arrived = local_copy[0]
    for begin, end in groups_of(total):
        joined = jnp.concatenate(
            [
                shuffled(squares[ORDER], arrived[:, i].reshape(count, channels))
                for i in range(begin, end)
            ],
            axis=0,
        )
        joined = attention_rows(
            joined, gain[layer, 1:2], squares, members
        ).astype(BF16)
        following = normalize(joined.astype(F32), gain[layer + 1, 0:1]).astype(BF16)
        for i in range(begin, end):
            span = slice((i - begin) * count, (i - begin + 1) * count)
            state[i] = joined[span]
            normed[i] = following[span]
            low[i] = following[span][:members]
            high[i] = following[span][count - members :]


def conv_tile_kernel(layer, first, last, rows, spans, members, cells, halo, *refs):
    pieces = len(spans)
    states, refs = refs[:pieces], refs[pieces:]
    normeds, refs = refs[:pieces], refs[pieces:]
    if halo:
        lows, refs = refs[:pieces], refs[pieces:]
        highs, refs = refs[:pieces], refs[pieces:]
        if len(cells) * members < states[0].shape[1]:
            inner, partial, refs = *refs[:2], refs[2:]
    if halo:
        gain, stacks, weight, out_hbm, out, semaphores = refs
        copies = Copies(semaphores)
    else:
        gain, stacks, weight, out, partial = refs
    squares = stacks.at[layer]
    end_cell = states[0].shape[1] // members - 1
    outputs = []
    count, channels = states[0].shape[1:]
    total = last - first
    size = len(cells) * members
    zeros = jnp.zeros((members, channels), BF16)

    def piece_of(row):
        for k, (begin, end) in enumerate(spans):
            if begin <= row < end:
                return k, row - begin

    def tap(row, cell):
        if not 0 <= row < rows:
            return zeros
        k, place = piece_of(row)
        if cell < 0:
            return lows[k][place]
        if cell * members == count:
            return highs[k][place]
        return normeds[k][place, cell * members : (cell + 1) * members]

    def held(row, cell):
        k, place = piece_of(row)
        return states[k][place, cell * members : (cell + 1) * members]

    def conv(begin, end, cells, sides):
        taps = [
            jnp.concatenate(
                [
                    jnp.concatenate(
                        [tap(first + i + di - 1, cell + dj - 1) for cell in cells], axis=0
                    )
                    for di in range(3)
                    for dj in sides
                ],
                axis=1,
            )
            for i in range(begin, end)
        ]
        return jnp.dot(
            jnp.concatenate(taps, axis=0),
            weight[:, sides.start : sides.stop].reshape(3 * len(sides) * channels, 2 * channels),
            preferred_element_type=F32,
        )

    for begin, end in groups_of(total, UNROLL * count // size):
        run = end - begin
        if not halo or size == count:
            conv_out = conv(begin, end, cells, range(3))
        else:
            beside = [
                conv(begin, end, cells[:1], range(1)).reshape(run, members, 2 * channels),
                conv(begin, end, cells[1:], range(2, 3)).reshape(run, members, 2 * channels),
            ]
            conv_out = jnp.concatenate(beside, axis=1) + partial[begin:end]
            conv_out = conv_out.reshape(run * size, 2 * channels)
        if not halo:
            own = conv(begin, end, (0,), range(1, 3))
            partial[begin:end, :members] = own.reshape(run, members, 2 * channels)
            own = conv(begin, end, (end_cell,), range(2))
            partial[begin:end, members:] = own.reshape(run, members, 2 * channels)
        joined = jnp.concatenate(
            [held(first + i, cell) for i in range(begin, end) for cell in cells], axis=0
        ).astype(F32)
        joined = (joined + gated(conv_out, channels)).astype(BF16).astype(F32)
        joined = attention_rows(
            joined, gain[layer, 1:2], squares, members
        ).astype(BF16)
        for i in range(begin, end):
            own = joined[(i - begin) * size : (i - begin + 1) * size]
            if halo:
                full = jnp.concatenate(
                    [own[:members], inner[i], own[members:]] if size < count else [own], axis=0
                )
                moved = shuffled(squares[ORDER], full)
                out[:, i] = moved.reshape(out.shape[0], out.shape[2], channels).astype(BF16)
            else:
                out[i] = own
        if halo:
            outputs.append(copies.start(out.at[:, begin:end], out_hbm.at[:, begin:end]))
    wait_all(outputs)


def place_kernel(first, earlier, *refs):
    if earlier:
        arrived, stacks, out_hbm, out, semaphores = refs[-5:]
    else:
        arrived_hbm, stacks, out_hbm, arrived, out, semaphores = refs
        copy = pltpu.make_async_copy(arrived_hbm, arrived, semaphores.at[31])
        copy.start()
        copy.wait()
    local, total, cols, channels = out.shape
    copies = Copies(semaphores)
    outputs = []
    for begin, end in groups_of(total, 2):
        for i in range(begin, end):
            moved = shuffled(stacks[0, FINAL], arrived[:, i].reshape(local * cols, channels))
            out[:, i] = moved.reshape(local, cols, channels).astype(BF16)
        outputs.append(
            copies.start(out.at[:, begin:end], out_hbm.at[:, first + begin : first + end])
        )
    wait_all(outputs)


def call(
    kernel, name, far, near, outs, scratch, flops, moved, transcendentals=0, aliases=None
):
    far = [pltpu.with_memory_space_constraint(x, pltpu.HBM) for x in far]
    near = [pltpu.with_memory_space_constraint(x, pltpu.VMEM) for x in near]
    anywhere, vmem = pl.BlockSpec(memory_space=pl.ANY), pl.BlockSpec(memory_space=pltpu.VMEM)
    scratch_shapes = [pltpu.VMEM(shape, dtype) for shape, dtype in scratch]
    if scratch:
        scratch_shapes.append(pltpu.SemaphoreType.DMA((32,)))
    return pl.pallas_call(
        kernel,
        out_shape=[
            (pltpu.VMEM if is_near else pltpu.HBM)(shape, dtype)
            for shape, dtype, is_near in outs
        ],
        in_specs=[anywhere] * len(far) + [vmem] * len(near),
        out_specs=[vmem if is_near else anywhere for _, _, is_near in outs],
        scratch_shapes=scratch_shapes,
        input_output_aliases=aliases or {},
        compiler_params=pltpu.CompilerParams(vmem_limit_bytes=VMEM_LIMIT),
        cost_estimate=pl.CostEstimate(
            flops=flops, bytes_accessed=moved, transcendentals=transcendentals
        ),
        name=name,
    )(*far, *near)


def chunks(rows):
    edges = [0, *(round(rows * cut / 16) for cut in CUTS), rows]
    inner = [edge - 1 for edge in edges[1:-1]]
    outer = [0, *inner, rows]
    return tuple(zip(edges, edges[1:])), tuple(zip(outer, outer[1:]))


def body(field, norm_gain, conv_weight, qkv_weight, out_weight):
    local, rows, cols, channels = field.shape
    devices = lax.axis_size("mem")
    width = cols // devices
    members = devices * local
    count = local * cols
    block = local * width
    to_message, to_tile, from_tile, to_slab = shuffles(devices, local, cols)
    taps = conv_weight.shape[1] * conv_weight.shape[2] * channels
    conv_shape = conv_weight.shape[1:]

    spans_in, spans_out = chunks(rows)
    square = ((count, count), BF16)

    def conv_slab(first, last):
        total = last - first
        held = min(last + 1, rows) - max(first - 1, 0)
        staging = last == rows
        far = [field, norm_gain, conv_weight, to_message]
        messages = (devices, total, block, channels)
        outs = [(messages, BF16, False)]
        scratch = [
            ((local, held, cols, channels), BF16),
            (norm_gain.shape, F32),
            (conv_shape, BF16),
            square,
            ((total + 2, 3, count, channels), BF16),
            (messages, BF16),
        ]
        if staging:
            far += [qkv_weight, out_weight, to_tile, from_tile, to_slab]
            outs += [
                (norm_gain.shape, F32, True),
                (conv_shape, BF16, True),
                ((BLOCKS, 6, channels, channels), BF16, True),
            ]
            scratch.append((qkv_weight.shape, BF16))
        return call(
            functools.partial(conv_slab_kernel, 0, first, last, staging),
            "conv_slab",
            far,
            [],
            outs,
            scratch,
            2 * total * count * taps * 2 * channels,
            4 * total * count * channels,
            total * count * channels,
        )

    def exchange(messages):
        return lax.all_to_all(messages, "mem", split_axis=0, concat_axis=0, tiled=True)

    tiles = [tile_of(d, devices) for d in range(devices)]
    owner = {t: d for d, t in enumerate(tiles)}
    rightward = [(owner[t], owner[t + 1]) for t in range(devices - 1)]
    leftward = [(target, source) for source, target in rightward]

    arrived = []
    for span in spans_in:
        messages, *staged = conv_slab(*span)
        arrived.append(exchange(messages))
    gain, later_weight, stacks = staged

    def attend(arrival, is_far):
        total = arrival.shape[1]
        whole, edge = (total, count, channels), (total, members, channels)
        return call(
            functools.partial(attend_kernel, 0, members),
            "attend",
            [arrival] if is_far else [],
            [gain, stacks] if is_far else [arrival, gain, stacks],
            [(shape, BF16, True) for shape in (whole, whole, edge, edge)],
            [(arrival.shape, BF16)] if is_far else [],
            2 * total * count * channels * 6 * channels,
            8 * total * count * channels,
            total * count * members * HEADS,
        )

    def conv_tile(first, last, spans, parts, cells, halo, inner=()):
        total = last - first
        operands = [p[k] for k in range(4 if halo else 2) for p in parts]
        operands += inner
        size = len(cells) * members
        shape = (devices, total, block, channels) if halo else (total, size, channels)
        return call(
            functools.partial(
                conv_tile_kernel, 1, first, last, rows, spans, members, cells, halo
            ),
            "conv_edges" if halo else "conv_inner",
            [],
            [*operands, gain, stacks, later_weight],
            [(shape, BF16, not halo)]
            + ([] if halo else [((total, 2 * members, 2 * channels), F32, True)]),
            [(shape, BF16)] if halo else [],
            2 * total * size * channels * (6 * channels + 2 * taps),
            8 * total * count * channels,
            total * size * members * HEADS,
        )

    def place(first, last, arrival, earlier):
        total = last - first
        return call(
            functools.partial(place_kernel, first, earlier is not None),
            "place",
            [arrival] if earlier is None else [earlier],
            [stacks] if earlier is None else [arrival, stacks],
            [((local, rows, cols, channels), BF16, False)],
            ([(arrival.shape, BF16)] if earlier is None else [])
            + [((local, total, cols, channels), BF16)],
            2 * total * count * count * channels,
            4 * total * count * channels,
            aliases={} if earlier is None else {0: 0},
        )[0]

    parts, returned = [], []

    def attend_chunk(k):
        state, normed, low, high = attend(arrived[k], k == 0)
        from_left = lax.ppermute(high, "mem", rightward)
        from_right = lax.ppermute(low, "mem", leftward)
        parts.append((state, normed, from_left, from_right))

    def tile_chunk(k):
        lo = max(k - 1, 0)
        rest = (*spans_out[k], spans_in[lo : k + 1], parts[lo : k + 1])
        if SPLIT_TILE and width > 2:
            inner = conv_tile(*rest, tuple(range(1, width - 1)), False)
            (messages,) = conv_tile(*rest, (0, width - 1), True, inner)
        else:
            (messages,) = conv_tile(*rest, tuple(range(width)), True)
        returned.append(exchange(messages))

    for k in range(len(spans_in) + AHEAD):
        if k < len(spans_in):
            attend_chunk(k)
        if k >= AHEAD:
            tile_chunk(k - AHEAD)
    result = None
    for span, arrival in zip(spans_out, returned):
        result = place(*span, arrival, result)
    return result


def solution(mesh):
    return jax.shard_map(
        body,
        mesh=mesh,
        in_specs=(P(("grp", "mem"), None, None, None), P(), P(), P(), P()),
        out_specs=P(("grp", "mem"), None, None, None),
        check_vma=False,
    )
```

```python
import functools

import jax
import jax.numpy as jnp
import numpy as np
from jax import lax
from jax.experimental import pallas as pl
from jax.experimental.pallas import tpu as pltpu
from jax.sharding import PartitionSpec as P

HEADS = 8
BLOCKS = 2
LANES = 128
epsilon = 1e-06
VMEM_LIMIT = 40 * 1024 * 1024
UNROLL = 5
CUTS = (7,)
AHEAD = 0
SPLIT_TILE = True
WQ_T, WV_T, WK, WOUT, ORDER, FINAL = range(6)

F32 = jnp.float32
BF16 = jnp.bfloat16


def tile_of(device, count):
    if count % 4:
        return device
    group, inner = device // 4, device % 4
    if group % 2:
        inner = (2, 3, 0, 1)[inner]
    return group * 4 + inner


def one_hot(sources):
    matrix = np.zeros((len(sources), len(sources)), np.float32)
    matrix[np.arange(len(sources)), np.asarray(sources)] = 1.0
    return jnp.asarray(matrix, BF16)


def shuffles(count, local, cols):
    width = cols // count
    members = count * local
    tiles = [tile_of(d, count) for d in range(count)]
    to_message = [
        m * cols + tiles[d] * width + c
        for d in range(count)
        for m in range(local)
        for c in range(width)
    ]
    to_slab = np.argsort(to_message)
    to_tile = [
        d * local * width + m * width + c
        for c in range(width)
        for d in range(count)
        for m in range(local)
    ]
    from_tile = np.argsort(to_tile)
    return one_hot(to_message), one_hot(to_tile), one_hot(from_tile), one_hot(to_slab)


def normalize(widened, gain):
    inverse = lax.rsqrt(jnp.mean(widened * widened, axis=-1, keepdims=True) + epsilon)
    return widened * inverse * gain


def gated(conv_out, channels):
    return conv_out[:, :channels] * jax.nn.sigmoid(conv_out[:, channels:])


def shuffled(matrix, rows):
    return jnp.dot(matrix, rows, preferred_element_type=F32)


def groups_of(total, most=UNROLL):
    pieces = -(-total // most)
    edges = [total * k // pieces for k in range(pieces + 1)]
    return [(edges[k], edges[k + 1]) for k in range(pieces)]


def attention_rows(state, gain, squares, members):
    total, channels = state.shape
    size = channels // HEADS
    group = LANES // size
    packed = LANES // members
    factor = float(np.log2(np.e) / np.sqrt(size))
    normed = normalize(state, gain).astype(BF16)
    keys = jnp.dot(normed, squares[WK], preferred_element_type=F32).astype(BF16)
    wqv_t = squares[WQ_T : WV_T + 1].reshape(2 * channels, channels)
    qv_t = lax.dot_general(
        wqv_t, normed, (((1,), (1,)), ((), ())), preferred_element_type=F32
    ).astype(BF16)
    lane = lax.broadcasted_iota(jnp.int32, (members, LANES), 1)
    masks = [
        ((lane >= k * members) & (lane < (k + 1) * members)).astype(F32).astype(BF16)
        for k in range(packed)
    ]
    spans = [slice(j * LANES, (j + 1) * LANES) for j in range(total // LANES)]
    quads = range(channels // LANES)
    scores = {}
    for j, span in enumerate(spans):
        for q in quads:
            blocks = []
            for h in range(group):
                row = q * LANES + h * size
                parts = [jnp.zeros((size, LANES), BF16)] * group
                parts[h] = qv_t[row : row + size, span]
                blocks.append(jnp.concatenate(parts, axis=1))
            scores[j, q] = jnp.dot(
                keys[span, q * LANES : (q + 1) * LANES],
                jnp.concatenate(blocks, axis=0),
                preferred_element_type=F32,
            )
    weights = {}
    for j in range(len(spans)):
        for q in quads:
            for h in range(group):
                square = scores[j, q][:, h * LANES : (h + 1) * LANES]
                dense = square[:members]
                for k in range(1, packed):
                    dense = jnp.where(
                        lane < k * members, dense, square[k * members : (k + 1) * members]
                    )
                top = jnp.max(dense, axis=0, keepdims=True)
                expo = jnp.exp2((dense - top) * factor)
                inverse = 1.0 / jnp.sum(expo, axis=0, keepdims=True)
                spread = expo.astype(BF16)
                if packed > 1:
                    spread = jnp.concatenate([spread * mask for mask in masks], axis=0)
                weights[j, q, h] = spread, inverse
    columns = []
    for j, span in enumerate(spans):
        pieces = []
        for q in quads:
            for h in range(0, group, 2):
                row = channels + q * LANES + h * size
                mixed = jnp.dot(
                    qv_t[row : row + 2 * size, span],
                    jnp.concatenate([weights[j, q, h + k][0] for k in range(2)], axis=1),
                    preferred_element_type=F32,
                )
                for k in range(2):
                    own = mixed[k * size : (k + 1) * size, k * LANES : (k + 1) * LANES]
                    pieces.append((own * weights[j, q, h + k][1]).astype(BF16))
        columns.append(jnp.concatenate(pieces, axis=0))
    attended_t = jnp.concatenate(columns, axis=1)
    update = lax.dot_general(
        attended_t, squares[WOUT], (((0,), (0,)), ((), ())), preferred_element_type=F32
    )
    return state + update


class Copies:
    def __init__(self, semaphores):
        self.semaphores = semaphores
        self.used = 0

    def start(self, source, target):
        copy = pltpu.make_async_copy(source, target, self.semaphores.at[self.used])
        self.used += 1
        copy.start()
        return copy


def wait_all(copies):
    for copy in copies:
        copy.wait()


def conv_slab_kernel(
    layer, first, last, staging, field_hbm, gain_hbm, weight_hbm, order_hbm, *refs,
):
    if staging:
        (qkv_hbm, wout_hbm, to_tile_hbm, from_tile_hbm, to_slab_hbm, out_hbm,
         later_gain, later_weight, stacks,
         field, gain, weight, order, padded, out, qkv, semaphores) = refs
    else:
        out_hbm, field, gain, weight, order, padded, out, semaphores = refs
    local, rows, cols, channels = field_hbm.shape
    count = local * cols
    copies = Copies(semaphores)
    low = max(first - 1, 0)
    groups = groups_of(last - first)
    gain_copy = copies.start(gain_hbm, gain)
    fields, late, staged = [], [], []
    ready = low
    for k, (begin, end) in enumerate(groups):
        needed = min(first + end + 1, rows)
        part = slice(ready - low, needed - low)
        fields.append(copies.start(field_hbm.at[:, ready:needed], field.at[:, part]))
        ready = needed
        if k == 0:
            late = [copies.start(weight_hbm.at[layer, di], weight.at[di]) for di in range(3)]
            order_copy = copies.start(order_hbm, order)
    if staging:
        staged = [
            copies.start(qkv_hbm, qkv),
            copies.start(gain_hbm, later_gain),
            copies.start(weight_hbm.at[layer + 1], later_weight),
            copies.start(wout_hbm.at[0], stacks.at[0, WOUT]),
            copies.start(wout_hbm.at[1], stacks.at[1, WOUT]),
            copies.start(to_tile_hbm, stacks.at[0, ORDER]),
            copies.start(from_tile_hbm, stacks.at[1, ORDER]),
            copies.start(to_slab_hbm, stacks.at[0, FINAL]),
        ]
    column = lax.broadcasted_iota(jnp.int32, (count, 1), 0) % cols
    zeros = jnp.zeros(padded.shape[1:], BF16)
    if first == 0:
        padded[0] = zeros
    if last == rows:
        padded[last - first + 1] = zeros
    gain_copy.wait()
    gain_row = gain[layer, 0:1]

    def prepare(row):
        widened = field[:, row - low].reshape(count, channels).astype(F32)
        normed = normalize(widened, gain_row)
        left = jnp.where(column == 0, 0.0, pltpu.roll(normed, 1, 0))
        right = jnp.where(column == cols - 1, 0.0, pltpu.roll(normed, count - 1, 0))
        slot = row - first + 1
        padded[slot, 0] = left.astype(BF16)
        padded[slot, 1] = normed.astype(BF16)
        padded[slot, 2] = right.astype(BF16)

    ready = low
    outputs = []
    for k, (begin, end) in enumerate(groups):
        needed = min(first + end + 1, rows)
        fields[k].wait()
        for row in range(ready, needed):
            prepare(row)
        ready = needed
        taps = [
            jnp.concatenate(
                [
                    jnp.concatenate([padded[i + di, dj] for dj in range(3)], axis=1)
                    for i in range(begin, end)
                ],
                axis=0,
            )
            for di in range(3)
        ]
        if k == 0:
            conv_out = 0.0
            for di in range(3):
                late[di].wait()
                conv_out += jnp.dot(
                    taps[di],
                    weight[di].reshape(3 * channels, 2 * channels),
                    preferred_element_type=F32,
                )
            order_copy.wait()
        else:
            conv_out = jnp.dot(
                jnp.concatenate(taps, axis=1),
                weight[...].reshape(9 * channels, 2 * channels),
                preferred_element_type=F32,
            )
        update = gated(conv_out, channels)
        for i in range(begin, end):
            widened = field[:, first + i - low].reshape(count, channels).astype(F32)
            part = update[(i - begin) * count : (i - begin + 1) * count]
            moved = shuffled(order[...], (widened + part).astype(BF16))
            out[:, i] = moved.reshape(out.shape[0], out.shape[2], channels).astype(BF16)
        outputs.append(copies.start(out.at[:, begin:end], out_hbm.at[:, begin:end]))
    if staging:
        wait_all(staged)
        for b in range(BLOCKS):
            stacks[b, WQ_T] = qkv[b, :, :channels].T
            stacks[b, WV_T] = qkv[b, :, 2 * channels :].T
            stacks[b, WK] = qkv[b, :, channels : 2 * channels]
    wait_all(outputs)


def attend_kernel(
    layer, members, arrived, gain, stacks, state, normed, low, high, *local_copy,
):
    total, count, channels = state.shape
    squares = stacks.at[layer]
    if local_copy:
        copy = pltpu.make_async_copy(arrived, local_copy[0], local_copy[1].at[0])
        copy.start()
        copy.wait()
        arrived = local_copy[0]
    for begin, end in groups_of(total):
        joined = jnp.concatenate(
            [
                shuffled(squares[ORDER], arrived[:, i].reshape(count, channels))
                for i in range(begin, end)
            ],
            axis=0,
        )
        joined = attention_rows(
            joined, gain[layer, 1:2], squares, members
        ).astype(BF16)
        following = normalize(joined.astype(F32), gain[layer + 1, 0:1]).astype(BF16)
        for i in range(begin, end):
            span = slice((i - begin) * count, (i - begin + 1) * count)
            state[i] = joined[span]
            normed[i] = following[span]
            low[i] = following[span][:members]
            high[i] = following[span][count - members :]


def conv_tile_kernel(layer, first, last, rows, spans, members, cells, halo, *refs):
    pieces = len(spans)
    states, refs = refs[:pieces], refs[pieces:]
    normeds, refs = refs[:pieces], refs[pieces:]
    if halo:
        lows, refs = refs[:pieces], refs[pieces:]
        highs, refs = refs[:pieces], refs[pieces:]
        if len(cells) * members < states[0].shape[1]:
            inner, partial, refs = *refs[:2], refs[2:]
    if halo:
        gain, stacks, weight, out_hbm, out, semaphores = refs
        copies = Copies(semaphores)
    else:
        gain, stacks, weight, out, partial = refs
    squares = stacks.at[layer]
    end_cell = states[0].shape[1] // members - 1
    outputs = []
    count, channels = states[0].shape[1:]
    total = last - first
    size = len(cells) * members
    zeros = jnp.zeros((members, channels), BF16)

    def piece_of(row):
        for k, (begin, end) in enumerate(spans):
            if begin <= row < end:
                return k, row - begin

    def tap(row, cell):
        if not 0 <= row < rows:
            return zeros
        k, place = piece_of(row)
        if cell < 0:
            return lows[k][place]
        if cell * members == count:
            return highs[k][place]
        return normeds[k][place, cell * members : (cell + 1) * members]

    def held(row, cell):
        k, place = piece_of(row)
        return states[k][place, cell * members : (cell + 1) * members]

    def conv(begin, end, cells, sides):
        taps = [
            jnp.concatenate(
                [
                    jnp.concatenate(
                        [tap(first + i + di - 1, cell + dj - 1) for cell in cells], axis=0
                    )
                    for di in range(3)
                    for dj in sides
                ],
                axis=1,
            )
            for i in range(begin, end)
        ]
        return jnp.dot(
            jnp.concatenate(taps, axis=0),
            weight[:, sides.start : sides.stop].reshape(3 * len(sides) * channels, 2 * channels),
            preferred_element_type=F32,
        )

    for begin, end in groups_of(total, UNROLL * count // size):
        run = end - begin
        if not halo or size == count:
            conv_out = conv(begin, end, cells, range(3))
        else:
            beside = [
                conv(begin, end, cells[:1], range(1)).reshape(run, members, 2 * channels),
                conv(begin, end, cells[1:], range(2, 3)).reshape(run, members, 2 * channels),
            ]
            conv_out = jnp.concatenate(beside, axis=1) + partial[begin:end]
            conv_out = conv_out.reshape(run * size, 2 * channels)
        if not halo:
            own = conv(begin, end, (0,), range(1, 3))
            partial[begin:end, :members] = own.reshape(run, members, 2 * channels)
            own = conv(begin, end, (end_cell,), range(2))
            partial[begin:end, members:] = own.reshape(run, members, 2 * channels)
        joined = jnp.concatenate(
            [held(first + i, cell) for i in range(begin, end) for cell in cells], axis=0
        ).astype(F32)
        joined = (joined + gated(conv_out, channels)).astype(BF16).astype(F32)
        joined = attention_rows(
            joined, gain[layer, 1:2], squares, members
        ).astype(BF16)
        for i in range(begin, end):
            own = joined[(i - begin) * size : (i - begin + 1) * size]
            if halo:
                full = jnp.concatenate(
                    [own[:members], inner[i], own[members:]] if size < count else [own], axis=0
                )
                moved = shuffled(squares[ORDER], full)
                out[:, i] = moved.reshape(out.shape[0], out.shape[2], channels).astype(BF16)
            else:
                out[i] = own
        if halo:
            outputs.append(copies.start(out.at[:, begin:end], out_hbm.at[:, begin:end]))
    wait_all(outputs)


def place_kernel(first, earlier, *refs):
    if earlier:
        arrived, stacks, out_hbm, out, semaphores = refs[-5:]
    else:
        arrived_hbm, stacks, out_hbm, arrived, out, semaphores = refs
        copy = pltpu.make_async_copy(arrived_hbm, arrived, semaphores.at[31])
        copy.start()
        copy.wait()
    local, total, cols, channels = out.shape
    copies = Copies(semaphores)
    outputs = []
    for begin, end in groups_of(total, 1):
        for i in range(begin, end):
            moved = shuffled(stacks[0, FINAL], arrived[:, i].reshape(local * cols, channels))
            out[:, i] = moved.reshape(local, cols, channels).astype(BF16)
        outputs.append(
            copies.start(out.at[:, begin:end], out_hbm.at[:, first + begin : first + end])
        )
    wait_all(outputs)


def call(
    kernel, name, far, near, outs, scratch, flops, moved, transcendentals=0, aliases=None
):
    far = [pltpu.with_memory_space_constraint(x, pltpu.HBM) for x in far]
    near = [pltpu.with_memory_space_constraint(x, pltpu.VMEM) for x in near]
    anywhere, vmem = pl.BlockSpec(memory_space=pl.ANY), pl.BlockSpec(memory_space=pltpu.VMEM)
    scratch_shapes = [pltpu.VMEM(shape, dtype) for shape, dtype in scratch]
    if scratch:
        scratch_shapes.append(pltpu.SemaphoreType.DMA((32,)))
    return pl.pallas_call(
        kernel,
        out_shape=[
            (pltpu.VMEM if is_near else pltpu.HBM)(shape, dtype)
            for shape, dtype, is_near in outs
        ],
        in_specs=[anywhere] * len(far) + [vmem] * len(near),
        out_specs=[vmem if is_near else anywhere for _, _, is_near in outs],
        scratch_shapes=scratch_shapes,
        input_output_aliases=aliases or {},
        compiler_params=pltpu.CompilerParams(vmem_limit_bytes=VMEM_LIMIT),
        cost_estimate=pl.CostEstimate(
            flops=flops, bytes_accessed=moved, transcendentals=transcendentals
        ),
        name=name,
    )(*far, *near)


def chunks(rows):
    edges = [0, *(round(rows * cut / 16) for cut in CUTS), rows]
    inner = [edge - 1 for edge in edges[1:-1]]
    outer = [0, *inner, rows]
    return tuple(zip(edges, edges[1:])), tuple(zip(outer, outer[1:]))


def body(field, norm_gain, conv_weight, qkv_weight, out_weight):
    local, rows, cols, channels = field.shape
    devices = lax.axis_size("mem")
    width = cols // devices
    members = devices * local
    count = local * cols
    block = local * width
    to_message, to_tile, from_tile, to_slab = shuffles(devices, local, cols)
    taps = conv_weight.shape[1] * conv_weight.shape[2] * channels
    conv_shape = conv_weight.shape[1:]

    spans_in, spans_out = chunks(rows)
    square = ((count, count), BF16)

    def conv_slab(first, last):
        total = last - first
        held = min(last + 1, rows) - max(first - 1, 0)
        staging = last == rows
        far = [field, norm_gain, conv_weight, to_message]
        messages = (devices, total, block, channels)
        outs = [(messages, BF16, False)]
        scratch = [
            ((local, held, cols, channels), BF16),
            (norm_gain.shape, F32),
            (conv_shape, BF16),
            square,
            ((total + 2, 3, count, channels), BF16),
            (messages, BF16),
        ]
        if staging:
            far += [qkv_weight, out_weight, to_tile, from_tile, to_slab]
            outs += [
                (norm_gain.shape, F32, True),
                (conv_shape, BF16, True),
                ((BLOCKS, 6, channels, channels), BF16, True),
            ]
            scratch.append((qkv_weight.shape, BF16))
        return call(
            functools.partial(conv_slab_kernel, 0, first, last, staging),
            "conv_slab",
            far,
            [],
            outs,
            scratch,
            2 * total * count * taps * 2 * channels,
            4 * total * count * channels,
            total * count * channels,
        )

    def exchange(messages):
        return lax.all_to_all(messages, "mem", split_axis=0, concat_axis=0, tiled=True)

    tiles = [tile_of(d, devices) for d in range(devices)]
    owner = {t: d for d, t in enumerate(tiles)}
    rightward = [(owner[t], owner[t + 1]) for t in range(devices - 1)]
    leftward = [(target, source) for source, target in rightward]

    arrived = []
    for span in spans_in:
        messages, *staged = conv_slab(*span)
        arrived.append(exchange(messages))
    gain, later_weight, stacks = staged

    def attend(arrival, is_far):
        total = arrival.shape[1]
        whole, edge = (total, count, channels), (total, members, channels)
        return call(
            functools.partial(attend_kernel, 0, members),
            "attend",
            [arrival] if is_far else [],
            [gain, stacks] if is_far else [arrival, gain, stacks],
            [(shape, BF16, True) for shape in (whole, whole, edge, edge)],
            [(arrival.shape, BF16)] if is_far else [],
            2 * total * count * channels * 6 * channels,
            8 * total * count * channels,
            total * count * members * HEADS,
        )

    def conv_tile(first, last, spans, parts, cells, halo, inner=()):
        total = last - first
        operands = [p[k] for k in range(4 if halo else 2) for p in parts]
        operands += inner
        size = len(cells) * members
        shape = (devices, total, block, channels) if halo else (total, size, channels)
        return call(
            functools.partial(
                conv_tile_kernel, 1, first, last, rows, spans, members, cells, halo
            ),
            "conv_edges" if halo else "conv_inner",
            [],
            [*operands, gain, stacks, later_weight],
            [(shape, BF16, not halo)]
            + ([] if halo else [((total, 2 * members, 2 * channels), F32, True)]),
            [(shape, BF16)] if halo else [],
            2 * total * size * channels * (6 * channels + 2 * taps),
            8 * total * count * channels,
            total * size * members * HEADS,
        )

    def place(first, last, arrival, earlier):
        total = last - first
        return call(
            functools.partial(place_kernel, first, earlier is not None),
            "place",
            [arrival] if earlier is None else [earlier],
            [stacks] if earlier is None else [arrival, stacks],
            [((local, rows, cols, channels), BF16, False)],
            ([(arrival.shape, BF16)] if earlier is None else [])
            + [((local, total, cols, channels), BF16)],
            2 * total * count * count * channels,
            4 * total * count * channels,
            aliases={} if earlier is None else {0: 0},
        )[0]

    parts, returned = [], []

    def attend_chunk(k):
        state, normed, low, high = attend(arrived[k], k == 0)
        from_left = lax.ppermute(high, "mem", rightward)
        from_right = lax.ppermute(low, "mem", leftward)
        parts.append((state, normed, from_left, from_right))

    def tile_chunk(k):
        lo = max(k - 1, 0)
        rest = (*spans_out[k], spans_in[lo : k + 1], parts[lo : k + 1])
        if SPLIT_TILE and width > 2:
            inner = conv_tile(*rest, tuple(range(1, width - 1)), False)
            (messages,) = conv_tile(*rest, (0, width - 1), True, inner)
        else:
            (messages,) = conv_tile(*rest, tuple(range(width)), True)
        returned.append(exchange(messages))

    for k in range(len(spans_in) + AHEAD):
        if k < len(spans_in):
            attend_chunk(k)
        if k >= AHEAD:
            tile_chunk(k - AHEAD)
    result = None
    for span, arrival in zip(spans_out, returned):
        result = place(*span, arrival, result)
    return result


def solution(mesh):
    return jax.shard_map(
        body,
        mesh=mesh,
        in_specs=(P(("grp", "mem"), None, None, None), P(), P(), P(), P()),
        out_specs=P(("grp", "mem"), None, None, None),
        check_vma=False,
    )
```
